256 devices in a mesh: blk: 8 (over y_hi, x), grp: 32 (over z, y_lo, core).
Axes of the slice: x: 4, y: 4 (y_hi: 2, y_lo: 2; y = y_hi * 2 + y_lo), z: 8, core: 2. Of those that a mesh axis runs over, the one named last changes fastest.
Arguments:
- picture_embedding_matrix: bfloat16 [32768, 1152], P(('blk', 'grp')), may hold values from -0.1875 to 0.1875
- caption_embedding_matrix: bfloat16 [32768, 1152], P(('blk', 'grp')), may hold values from -0.1875 to 0.1875
- score_multiplier: float32 [1], replicated, may hold values from 20 to 80
- sigmoid_offset_array: float32 [1], replicated, may hold values from -5 to -3
Outputs:
- visual_steepness: float32 [32768, 1152], P(('blk', 'grp'))
- grad_text: float32 [32768, 1152], P(('blk', 'grp'))
The draws below stay inside these ranges and needn't reach their ends.
All inputs are finite; a program needn't handle non-finite values.
Results may differ from the reference program's by a relative error of at most 0.0015.
Values may be sent and summed in bfloat16 or wider, within the bound.
A program may use at most 128 MiB of HBM per device.

```python
import math
import jax
import jax.numpy as jnp

D = 1152
TOK_DEV = 128
WINDOW = 2
BATCH = 32768
N_BLK = 8
N_GRP = 32


def steps_of(stream_key, extent, pieces, low, top_value):
    def one(dim, blocks):
        steps = jax.random.uniform(jax.random.fold_in(jax.random.fold_in(stream_key, 6), dim), (blocks,), jnp.float32, low / len(pieces), top_value / len(pieces))
        return jnp.repeat(jnp.exp(steps), extent[dim] // blocks).reshape((-1,) + (1,) * (len(extent) - dim - 1))

    loudness = one(*pieces[0])
    for cut in pieces[1:]:
        loudness = loudness * one(*cut)
    return loudness


def scatter_about(rng, dims, scale, most, shards=(), held_as=jnp.bfloat16):
    entries = scale * jax.random.normal(rng, dims, jnp.float32)
    if shards:
        entries = entries * steps_of(rng, dims, shards, -0.22, 0.18)
    return jnp.clip(entries, -most, most).astype(held_as)


def setup_inputs(seed: int = 0) -> dict:
    arg_keys = jax.random.split(jax.random.key(seed), 5)
    picture_embedding_matrix = scatter_about(arg_keys[0], (BATCH, D), 0.03, 0.1875, ((0, 256),))
    caption_embedding_matrix = scatter_about(arg_keys[1], (BATCH, D), 0.03, 0.1875, ((0, 256),))
    score_multiplier = jnp.clip(jnp.exp(jax.random.uniform(arg_keys[2], (1,), jnp.float32, math.log(20.0), math.log(80.0))), 20.0, 80.0)
    sigmoid_offset_array = jnp.clip(jax.random.uniform(arg_keys[3], (1,), jnp.float32, -5.0, -3.0), -5.0, -3.0)
    return dict(picture_embedding_matrix=picture_embedding_matrix, caption_embedding_matrix=caption_embedding_matrix, score_multiplier=score_multiplier, sigmoid_offset_array=sigmoid_offset_array)


def reference(picture_embedding_matrix, caption_embedding_matrix, score_multiplier, sigmoid_offset_array):
    pairs_per_set = TOK_DEV * N_GRP
    image_batch = picture_embedding_matrix.reshape(N_BLK, pairs_per_set, D)
    texts = caption_embedding_matrix.reshape(N_BLK, pairs_per_set, D)
    inverse_warmth = score_multiplier[0]
    additive_shift_bias = sigmoid_offset_array[0]
    identity = jnp.eye(pairs_per_set, dtype=jnp.float32)
    visual_steepness = [jnp.zeros((pairs_per_set, D), jnp.float32) for sender_position in range(N_BLK)]
    grad_text = [jnp.zeros((pairs_per_set, D), jnp.float32) for sender_position in range(N_BLK)]
    for sender_position in range(N_BLK):
        visual_tile = image_batch[sender_position]
        for hop_index in range(WINDOW):
            target = (sender_position - hop_index) % N_BLK
            wording_tile = texts[target]
            similarity_scores = inverse_warmth * jnp.dot(visual_tile, wording_tile.T, preferred_element_type=jnp.float32) + additive_shift_bias
            weights = jax.nn.sigmoid(similarity_scores)
            if hop_index == 0:
                weights = weights - identity
            weighting_entries = weights.astype(jnp.bfloat16)
            visual_steepness[sender_position] = visual_steepness[sender_position] + inverse_warmth * jnp.dot(weighting_entries, wording_tile, preferred_element_type=jnp.float32)
            partial_sum = inverse_warmth * jnp.dot(weighting_entries.T, visual_tile, preferred_element_type=jnp.float32)
            grad_text[target] = grad_text[target] + partial_sum
    return jnp.concatenate(visual_steepness, axis=0), jnp.concatenate(grad_text, axis=0)
```

```python
import functools

import jax
import jax.numpy as jnp
from jax import lax
from jax.experimental import pallas as pl
from jax.experimental.pallas import tpu as pltpu
from jax.sharding import PartitionSpec as P

MESH = pl.DeviceIdType.MESH
LIFT = 2.0**18
TINY = 1e-37
HALF = 64
ROWS = 128
NT = (((1,), (1,)), ((), ()))
TN = (((0,), (0,)), ((), ()))

Z_RIGHT, Z_LEFT = 0, 8
S_RIGHT, S_LEFT = 16, 24
T_CORE, T_Y, T_X = 32, 36, 38
G_CORE, G_Y, G_X = 40, 42, 44
N_SEM = 45


def code(v):
    w = v * LIFT
    w = w * jnp.abs(w)
    w = w * jnp.abs(w)
    return w.astype(jnp.bfloat16)


def decode(u):
    u = u.astype(jnp.float32)
    r = lax.rsqrt(lax.rsqrt(jnp.maximum(jnp.abs(u), TINY))) * (1.0 / LIFT)
    return jnp.where(u < 0.0, -r, r)


def kernel(
    x_ref, t_ref, scale_ref, bias_ref, vis_ref, txt_ref,
    xb, tb, cb, vp, gp, sl, sr, rl, rr, core_out, core_in, y_out, y_in, x_out, x_in, ss, rs, own,
):
    blk = lax.axis_index("blk")
    grp = lax.axis_index("grp")
    z, y, core = grp // 4, (grp // 2) % 2, grp % 2
    right = (blk, ((z + 1) % 8) * 4 + y * 2 + core)
    left = (blk, ((z + 7) % 8) * 4 + y * 2 + core)
    across = (blk, z * 4 + (1 - y) * 2 + core)
    sibling = (blk, z * 4 + y * 2 + (1 - core))
    flip_down = 1 - (blk % 4 + 3) // 4
    up_blk = (blk + 1) % 8
    flip_up = 1 - (up_blk % 4 + 3) // 4
    down = ((blk + 7) % 8, z * 4 + ((y + flip_down) % 2) * 2 + core)
    up = (up_blk, z * 4 + ((y + flip_up) % 2) * 2 + core)

    own_image = pltpu.make_async_copy(x_ref, xb.at[pl.ds(0, ROWS)], own.at[0])
    own_text = pltpu.make_async_copy(t_ref, tb.at[pl.ds(0, ROWS)], own.at[1])
    own_image.start()
    own_text.start()

    barrier = pltpu.get_barrier_semaphore()
    for other in (right, left, across, sibling, down, up):
        pl.semaphore_signal(barrier, inc=1, device_id=other, device_id_type=MESH)
    pl.semaphore_wait(barrier, 6)

    copies = []

    def send(k, src, dst, device):
        copy = pltpu.make_async_remote_copy(
            src_ref=src, dst_ref=dst, send_sem=ss.at[k], recv_sem=rs.at[k],
            device_id=device, device_id_type=MESH,
        )
        copy.start()
        copies.append(copy)
        return copy

    low, high = pl.ds(0, HALF), pl.ds(HALF, HALF)

    def from_left(i):
        return pl.ds(ROWS * i, HALF)

    def from_right(i):
        return pl.ds(ROWS * i + HALF, HALF)

    def text(h, yy, cc):
        return pl.ds(512 * h + 256 * yy + 128 * cc, 128)

    zr, zl, tc = {}, {}, {}
    zr[1] = send(Z_RIGHT + 1, x_ref.at[low], xb.at[from_left(1)], right)
    zl[1] = send(Z_LEFT + 1, x_ref.at[high], xb.at[from_right(1)], left)
    ty0 = send(T_Y, t_ref, tb.at[text(0, 1, 0)], across)
    tx = send(T_X, t_ref, tb.at[text(1, 0, 0)], up)
    tc[0, 0] = send(T_CORE, t_ref, tb.at[text(0, 0, 1)], sibling)
    zr[2] = send(Z_RIGHT + 2, x_ref.at[high], xb.at[from_left(2)], right)
    zl[2] = send(Z_LEFT + 2, x_ref.at[low], xb.at[from_right(2)], left)

    scale = scale_ref[0]
    bias = bias_ref[0]

    def arrive(i):
        zr[i].wait_recv()
        zl[i].wait_recv()
        if i + 2 <= 7:
            zr[i + 2] = send(Z_RIGHT + i + 2, xb.at[from_left(i)], xb.at[from_left(i + 2)], right)
            zl[i + 2] = send(Z_LEFT + i + 2, xb.at[from_right(i)], xb.at[from_right(i + 2)], left)

    def coefficients(start, rows, h):
        x = xb[start : start + rows, :]

        def tile(n, carry):
            cols = pl.ds(pl.multiple_of(n * 256, 256), 256)
            dots = lax.dot_general(x, tb[cols, :], NT, preferred_element_type=jnp.float32)
            away = jnp.minimum(dots * (-scale) - bias, 87.0)
            c = 1.0 / (1.0 + jnp.exp(away))
            if start == 0 and h == 0:
                row = lax.broadcasted_iota(jnp.int32, c.shape, 0)
                col = lax.broadcasted_iota(jnp.int32, c.shape, 1) + n * 256
                c = jnp.where((row == col) & (row < ROWS), c - 1.0, c)
            cb[start : start + rows, cols] = c.astype(jnp.bfloat16)
            return carry

        lax.fori_loop(2 * h, 2 * h + 2, tile, 0)

    def image_terms(start, rows):
        def tile(n, carry):
            cols = pl.ds(pl.multiple_of(n * 384, 384), 384)
            vp[start : start + rows, cols] = jnp.dot(
                cb[start : start + rows, :], tb[:, cols], preferred_element_type=jnp.float32
            )
            return carry

        lax.fori_loop(0, 3, tile, 0)

    def text_terms(h):
        def tile(m, carry):
            cols = pl.ds(pl.multiple_of(m * 256, 256), 256)
            gp[cols, :] = lax.dot_general(cb[:, cols], xb[...], TN, preferred_element_type=jnp.float32)
            return carry

        lax.fori_loop(2 * h, 2 * h + 2, tile, 0)

    vl, vr = {}, {}

    def pass_on(i):
        to_left = vp[ROWS * i : ROWS * i + HALF, :]
        to_right = vp[ROWS * i + HALF : ROWS * (i + 1), :]
        if i <= 5:
            vl[i + 2].wait_recv()
            to_left = to_left + decode(rl[i + 2])
        sl[i] = code(to_left)
        vl[i] = send(S_LEFT + i, sl.at[i], rl.at[i], left)
        if i <= 5:
            vr[i + 2].wait_recv()
            to_right = to_right + decode(rr[i + 2])
        sr[i] = code(to_right)
        vr[i] = send(S_RIGHT + i, sr.at[i], rr.at[i], right)

    def code_rows(dst, src, src_start, count):
        def some(k, carry):
            at = pl.multiple_of(k * 64, 64)
            dst[pl.ds(at, 64), :] = code(src[pl.ds(src_start + at, 64), :])
            return carry

        lax.fori_loop(0, count // 64, some, 0)

    gc = {}

    def text_to_sibling(h):
        for yy in range(2):
            code_rows(core_out.at[h, yy], gp, 512 * h + 256 * yy + 128, 128)
        gc[h] = send(G_CORE + h, core_out.at[h], core_in.at[h], sibling)

    gy = {}

    def text_across(h):
        gc[h].wait_recv()

        def some(k, carry):
            at = pl.ds(pl.multiple_of(k * 64, 64), 64)
            far = pl.ds(512 * h + 256 + pl.multiple_of(k * 64, 64), 64)
            y_out[h, at, :] = code(gp[far, :] + decode(core_in[h, 1, at, :]))
            return carry

        lax.fori_loop(0, 2, some, 0)
        gy[h] = send(G_Y + h, y_out.at[h], y_in.at[h], across)

    def text_sum(h, at, near):
        return gp[near, :] + decode(core_in[h, 0, at, :]) + decode(y_in[h, at, :])

    arrive(1)
    ty0.wait_recv()
    tc[0, 1] = send(T_CORE + 1, tb.at[text(0, 1, 0)], tb.at[text(0, 1, 1)], sibling)
    tx.wait_recv()
    ty1 = send(T_Y + 1, tb.at[text(1, 0, 0)], tb.at[text(1, 1, 0)], across)
    tc[1, 0] = send(T_CORE + 2, tb.at[text(1, 0, 0)], tb.at[text(1, 0, 1)], sibling)
    arrive(2)
    own_text.wait()
    own_image.wait()
    tc[0, 0].wait_recv()
    tc[0, 1].wait_recv()
    coefficients(0, 256, 0)
    arrive(3)
    coefficients(256, 256, 0)
    arrive(4)
    ty1.wait_recv()
    tc[1, 1] = send(T_CORE + 3, tb.at[text(1, 1, 0)], tb.at[text(1, 1, 1)], sibling)
    tc[1, 0].wait_recv()
    tc[1, 1].wait_recv()
    coefficients(0, 256, 1)
    arrive(5)
    coefficients(256, 256, 1)
    coefficients(512, 256, 0)
    coefficients(512, 256, 1)
    arrive(6)
    coefficients(768, 128, 0)
    coefficients(768, 128, 1)
    image_terms(768, 128)
    pass_on(6)
    image_terms(512, 256)
    arrive(7)
    coefficients(896, 128, 0)
    coefficients(896, 128, 1)
    image_terms(896, 128)
    pass_on(7)
    text_terms(1)
    text_to_sibling(1)
    pass_on(4)
    text_terms(0)
    text_to_sibling(0)
    pass_on(5)
    text_across(1)
    text_across(0)
    image_terms(256, 256)
    pass_on(2)
    gy[1].wait_recv()
    for k in range(2):
        at = pl.ds(64 * k, 64)
        x_out[at, :] = code(text_sum(1, at, pl.ds(512 + 64 * k, 64)))
    gx = send(G_X, x_out, x_in, down)
    pass_on(3)
    image_terms(0, 256)
    gy[0].wait_recv()
    for k in range(2):
        at = pl.ds(64 * k, 64)
        gp[at, :] = text_sum(0, at, at)
    pass_on(1)
    gx.wait_recv()
    for k in range(2):
        at = pl.ds(64 * k, 64)
        txt_ref[at, :] = scale * (gp[at, :] + decode(x_in[at, :]))
    vl[2].wait_recv()
    vr[2].wait_recv()
    vp[low, :] = vp[low, :] + decode(rr[2])
    vp[high, :] = vp[high, :] + decode(rl[2])
    vl[1].wait_recv()
    vr[1].wait_recv()
    vis_ref[low, :] = scale * (vp[low, :] + decode(rl[1]))
    vis_ref[high, :] = scale * (vp[high, :] + decode(rr[1]))
    for copy in copies:
        copy.wait_send()


def per_device(images, texts, scale, bias):
    rows, width = images.shape
    bf16, f32 = jnp.bfloat16, jnp.float32
    out = jax.ShapeDtypeStruct((rows, width), f32)
    vmem = pl.BlockSpec(memory_space=pltpu.VMEM)
    hbm = pl.BlockSpec(memory_space=pltpu.HBM)
    smem = pl.BlockSpec(memory_space=pltpu.SMEM)
    return pl.pallas_call(
        kernel,
        out_shape=(out, out),
        in_specs=[hbm, hbm, smem, smem],
        out_specs=(vmem, vmem),
        scratch_shapes=[
            pltpu.VMEM((1024, width), bf16),
            pltpu.VMEM((1024, width), bf16),
            pltpu.VMEM((1024, 1024), bf16),
            pltpu.VMEM((1024, width), f32),
            pltpu.VMEM((1024, width), f32),
            pltpu.VMEM((8, HALF, width), bf16),
            pltpu.VMEM((8, HALF, width), bf16),
            pltpu.VMEM((8, HALF, width), bf16),
            pltpu.VMEM((8, HALF, width), bf16),
            pltpu.VMEM((2, 2, ROWS, width), bf16),
            pltpu.VMEM((2, 2, ROWS, width), bf16),
            pltpu.VMEM((2, ROWS, width), bf16),
            pltpu.VMEM((2, ROWS, width), bf16),
            pltpu.VMEM((ROWS, width), bf16),
            pltpu.VMEM((ROWS, width), bf16),
            pltpu.SemaphoreType.DMA((N_SEM,)),
            pltpu.SemaphoreType.DMA((N_SEM,)),
            pltpu.SemaphoreType.DMA((2,)),
        ],
        compiler_params=pltpu.CompilerParams(
            collective_id=0, has_side_effects=True, vmem_limit_bytes=48 * 1024 * 1024
        ),
        cost_estimate=pl.CostEstimate(
            flops=6 * 1024 * 1024 * width, bytes_accessed=12 * rows * width, transcendentals=2 * 1024 * 1024
        ),
    )(pltpu.with_memory_space_constraint(images, pltpu.HBM), pltpu.with_memory_space_constraint(texts, pltpu.HBM), scale, bias)


def solution(mesh):
    spec = P(("blk", "grp"), None)
    return jax.shard_map(
        per_device,
        mesh=mesh,
        in_specs=(spec, spec, P(), P()),
        out_specs=(spec, spec),
        check_vma=False,
    )
```

```python
import functools

import jax
import jax.numpy as jnp
from jax import lax
from jax.experimental import pallas as pl
from jax.experimental.pallas import tpu as pltpu
from jax.sharding import PartitionSpec as P

MESH = pl.DeviceIdType.MESH
LIFT = 2.0**18
TINY = 1e-37
LOG2E = 1.4426950408889634
HALF = 64
ROWS = 128
NT = (((1,), (1,)), ((), ()))
TN = (((0,), (0,)), ((), ()))

Z_RIGHT, Z_LEFT = 0, 8
S_RIGHT, S_LEFT = 16, 32
T_CORE, T_Y, T_X = 48, 52, 54
G_CORE, G_Y, G_X = 55, 59, 63
N_SEM = 65
PIECES = 2


def code(v):
    w = v * LIFT
    w = w * jnp.abs(w)
    w = w * jnp.abs(w)
    return w.astype(jnp.bfloat16)


def decode(u):
    u = u.astype(jnp.float32)
    r = lax.rsqrt(lax.rsqrt(jnp.maximum(jnp.abs(u), TINY))) * (1.0 / LIFT)
    return jnp.where(u < 0.0, -r, r)


def kernel(
    x_ref, t_ref, scale_ref, bias_ref, vis_ref, txt_ref,
    xb, tb, cb, vp, gp, sl, sr, rl, rr, core_out, core_in, y_out, y_in, x_out, x_in, ss, rs, own,
):
    blk = lax.axis_index("blk")
    grp = lax.axis_index("grp")
    z, y, core = grp // 4, (grp // 2) % 2, grp % 2
    right = (blk, ((z + 1) % 8) * 4 + y * 2 + core)
    left = (blk, ((z + 7) % 8) * 4 + y * 2 + core)
    across = (blk, z * 4 + (1 - y) * 2 + core)
    sibling = (blk, z * 4 + y * 2 + (1 - core))
    flip_down = 1 - (blk % 4 + 3) // 4
    up_blk = (blk + 1) % 8
    flip_up = 1 - (up_blk % 4 + 3) // 4
    down = ((blk + 7) % 8, z * 4 + ((y + flip_down) % 2) * 2 + core)
    up = (up_blk, z * 4 + ((y + flip_up) % 2) * 2 + core)

    own_image = pltpu.make_async_copy(x_ref, xb.at[pl.ds(0, ROWS)], own.at[0])
    own_text = pltpu.make_async_copy(t_ref, tb.at[pl.ds(0, ROWS)], own.at[1])
    own_image.start()
    own_text.start()

    barrier = pltpu.get_barrier_semaphore()
    for other in (right, left, across, sibling, down, up):
        pl.semaphore_signal(barrier, inc=1, device_id=other, device_id_type=MESH)
    pl.semaphore_wait(barrier, 6)

    copies = []

    def send(k, src, dst, device):
        copy = pltpu.make_async_remote_copy(
            src_ref=src, dst_ref=dst, send_sem=ss.at[k], recv_sem=rs.at[k],
            device_id=device, device_id_type=MESH,
        )
        copy.start()
        copies.append(copy)
        return copy

    low, high = pl.ds(0, HALF), pl.ds(HALF, HALF)

    def from_left(i):
        return pl.ds(ROWS * i, HALF)

    def from_right(i):
        return pl.ds(ROWS * i + HALF, HALF)

    def text(h, yy, cc):
        return pl.ds(512 * h + 256 * yy + 128 * cc, 128)

    zr, zl, tc = {}, {}, {}
    zr[1] = send(Z_RIGHT + 1, x_ref.at[low], xb.at[from_left(1)], right)
    zl[1] = send(Z_LEFT + 1, x_ref.at[high], xb.at[from_right(1)], left)
    ty0 = send(T_Y, t_ref, tb.at[text(0, 1, 0)], across)
    tx = send(T_X, t_ref, tb.at[text(1, 0, 0)], up)
    tc[0, 0] = send(T_CORE, t_ref, tb.at[text(0, 0, 1)], sibling)
    zr[1].wait_send()
    zl[1].wait_send()
    zr[2] = send(Z_RIGHT + 2, x_ref.at[high], xb.at[from_left(2)], right)
    zl[2] = send(Z_LEFT + 2, x_ref.at[low], xb.at[from_right(2)], left)

    scale = scale_ref[0]
    slope = scale * (-LOG2E)
    shift = bias_ref[0] * LOG2E

    def arrive(i):
        zr[i].wait_recv()
        zl[i].wait_recv()
        if i + 2 <= 7:
            zr[i + 2] = send(Z_RIGHT + i + 2, xb.at[from_left(i)], xb.at[from_left(i + 2)], right)
            zl[i + 2] = send(Z_LEFT + i + 2, xb.at[from_right(i)], xb.at[from_right(i + 2)], left)

    def coefficients(start, rows, h):
        x = xb[start : start + rows, :]

        def tile(n, carry):
            texts = pl.ds(pl.multiple_of(n * 256, 256), 256)
            dots = lax.dot_general(tb[texts, :], x, NT, preferred_element_type=jnp.float32)
            away = 1.0 + jnp.exp2(jnp.minimum(dots * slope - shift, 126.0))
            c = pl.reciprocal(away, approx=True)
            c = c * (2.0 - away * c)
            if start == 0 and h == 0:
                row = lax.broadcasted_iota(jnp.int32, c.shape, 0) + n * 256
                col = lax.broadcasted_iota(jnp.int32, c.shape, 1)
                c = jnp.where((row == col) & (row < ROWS), c - 1.0, c)
            cb[texts, start : start + rows] = c.astype(jnp.bfloat16)
            return carry

        lax.fori_loop(2 * h, 2 * h + 2, tile, 0)

    def image_terms(start, rows, first, last):
        texts = pl.ds(512 * first, 512 * (last - first))
        term = lax.dot_general(
            cb[texts, start : start + rows], tb[texts, :], TN, preferred_element_type=jnp.float32
        )
        if first > 0:
            term = vp[start : start + rows, :] + term
        vp[start : start + rows, :] = term

    def text_terms(h):
        texts = pl.ds(512 * h, 512)
        gp[texts, :] = jnp.dot(cb[texts, :], xb[...], preferred_element_type=jnp.float32)

    vl, vr = {}, {}

    def pass_on(i):
        for p in range(PIECES):
            part = pl.ds(p * HALF // PIECES, HALF // PIECES)
            for way, (sent, out, came, to, k) in enumerate(
                ((vl, sl, rl, left, S_LEFT), (vr, sr, rr, right, S_RIGHT))
            ):
                total = vp[pl.ds(ROWS * i + HALF * way + p * HALF // PIECES, HALF // PIECES), :]
                if i <= 5:
                    sent[i + 2, p].wait_recv()
                    total = total + decode(came[i + 2, part, :])
                out[i, part, :] = code(total)
                sent[i, p] = send(k + PIECES * i + p, out.at[i, part], came.at[i, part], to)

    def code_rows(dst, src, src_start, count):
        def some(k, carry):
            at = pl.multiple_of(k * 64, 64)
            dst[pl.ds(at, 64), :] = code(src[pl.ds(src_start + at, 64), :])
            return carry

        lax.fori_loop(0, count // 64, some, 0)

    gc = {}

    def text_to_sibling(h):
        for yy in (1, 0):
            code_rows(core_out.at[h, yy], gp, 512 * h + 256 * yy + 128, 128)
            gc[h, yy] = send(G_CORE + 2 * h + yy, core_out.at[h, yy], core_in.at[h, yy], sibling)

    gy = {}

    def text_across(h):
        gc[h, 1].wait_recv()
        for k in range(2):
            at = pl.ds(64 * k, 64)
            y_out[h, at, :] = code(gp[pl.ds(512 * h + 256 + 64 * k, 64), :] + decode(core_in[h, 1, at, :]))
            gy[h, k] = send(G_Y + 2 * h + k, y_out.at[h, at], y_in.at[h, at], across)

    def text_sum(h, k):
        at = pl.ds(64 * k, 64)
        if k == 0:
            gc[h, 0].wait_recv()
        gy[h, k].wait_recv()
        near = gp[pl.ds(512 * h + 64 * k, 64), :]
        return near + decode(core_in[h, 0, at, :]) + decode(y_in[h, at, :])

    arrive(1)
    ty0.wait_recv()
    tc[0, 1] = send(T_CORE + 1, tb.at[text(0, 1, 0)], tb.at[text(0, 1, 1)], sibling)
    tx.wait_recv()
    ty1 = send(T_Y + 1, tb.at[text(1, 0, 0)], tb.at[text(1, 1, 0)], across)
    tc[1, 0] = send(T_CORE + 2, tb.at[text(1, 0, 0)], tb.at[text(1, 0, 1)], sibling)
    arrive(2)
    own_text.wait()
    own_image.wait()
    tc[0, 0].wait_recv()
    tc[0, 1].wait_recv()
    coefficients(0, 256, 0)
    arrive(3)
    coefficients(256, 256, 0)
    image_terms(0, 512, 0, 1)
    arrive(4)
    ty1.wait_recv()
    tc[1, 1] = send(T_CORE + 3, tb.at[text(1, 1, 0)], tb.at[text(1, 1, 1)], sibling)
    coefficients(512, 128, 0)
    tc[1, 0].wait_recv()
    tc[1, 1].wait_recv()
    coefficients(0, 256, 1)
    arrive(5)
    coefficients(256, 256, 1)
    coefficients(640, 128, 0)
    coefficients(512, 256, 1)
    arrive(6)
    coefficients(768, 128, 0)
    coefficients(768, 128, 1)
    image_terms(768, 128, 0, 2)
    pass_on(6)
    image_terms(512, 256, 0, 2)
    arrive(7)
    coefficients(896, 128, 0)
    coefficients(896, 128, 1)
    image_terms(896, 128, 0, 2)
    pass_on(7)
    text_terms(1)
    text_to_sibling(1)
    pass_on(4)
    text_across(1)
    text_terms(0)
    text_to_sibling(0)
    pass_on(5)
    text_across(0)
    image_terms(0, 512, 1, 2)
    pass_on(2)
    gx = {}
    for k in range(2):
        at = pl.ds(64 * k, 64)
        x_out[at, :] = code(text_sum(1, k))
        gx[k] = send(G_X + k, x_out.at[at], x_in.at[at], down)
    pass_on(3)
    pass_on(1)
    for p in range(PIECES):
        vl[2, p].wait_recv()
        vr[2, p].wait_recv()
    vp[low, :] = vp[low, :] + decode(rr[2])
    vp[high, :] = vp[high, :] + decode(rl[2])
    for k in range(2):
        gp[pl.ds(64 * k, 64), :] = text_sum(0, k)
    for k in range(2):
        at = pl.ds(64 * k, 64)
        gx[k].wait_recv()
        txt_ref[at, :] = scale * (gp[at, :] + decode(x_in[at, :]))
    for p in range(PIECES):
        vl[1, p].wait_recv()
        vr[1, p].wait_recv()
    vis_ref[low, :] = scale * (vp[low, :] + decode(rl[1]))
    vis_ref[high, :] = scale * (vp[high, :] + decode(rr[1]))
    for copy in copies:
        if copy is not zr[1] and copy is not zl[1]:
            copy.wait_send()


def per_device(images, texts, scale, bias):
    rows, width = images.shape
    bf16, f32 = jnp.bfloat16, jnp.float32
    out = jax.ShapeDtypeStruct((rows, width), f32)
    vmem = pl.BlockSpec(memory_space=pltpu.VMEM)
    hbm = pl.BlockSpec(memory_space=pltpu.HBM)
    smem = pl.BlockSpec(memory_space=pltpu.SMEM)
    return pl.pallas_call(
        kernel,
        out_shape=(out, out),
        in_specs=[hbm, hbm, smem, smem],
        out_specs=(vmem, vmem),
        scratch_shapes=[
            pltpu.VMEM((1024, width), bf16),
            pltpu.VMEM((1024, width), bf16),
            pltpu.VMEM((1024, 1024), bf16),
            pltpu.VMEM((1024, width), f32),
            pltpu.VMEM((1024, width), f32),
            pltpu.VMEM((8, HALF, width), bf16),
            pltpu.VMEM((8, HALF, width), bf16),
            pltpu.VMEM((8, HALF, width), bf16),
            pltpu.VMEM((8, HALF, width), bf16),
            pltpu.VMEM((2, 2, ROWS, width), bf16),
            pltpu.VMEM((2, 2, ROWS, width), bf16),
            pltpu.VMEM((2, ROWS, width), bf16),
            pltpu.VMEM((2, ROWS, width), bf16),
            pltpu.VMEM((ROWS, width), bf16),
            pltpu.VMEM((ROWS, width), bf16),
            pltpu.SemaphoreType.DMA((N_SEM,)),
            pltpu.SemaphoreType.DMA((N_SEM,)),
            pltpu.SemaphoreType.DMA((2,)),
        ],
        compiler_params=pltpu.CompilerParams(
            collective_id=0, has_side_effects=True, vmem_limit_bytes=48 * 1024 * 1024
        ),
        cost_estimate=pl.CostEstimate(
            flops=6 * 1024 * 1024 * width, bytes_accessed=12 * rows * width, transcendentals=2 * 1024 * 1024
        ),
    )(pltpu.with_memory_space_constraint(images, pltpu.HBM), pltpu.with_memory_space_constraint(texts, pltpu.HBM), scale, bias)


def solution(mesh):
    spec = P(("blk", "grp"), None)
    return jax.shard_map(
        per_device,
        mesh=mesh,
        in_specs=(spec, spec, P(), P()),
        out_specs=(spec, spec),
        check_vma=False,
    )
```

```python
import functools

import jax
import jax.numpy as jnp
from jax import lax
from jax.experimental import pallas as pl
from jax.experimental.pallas import tpu as pltpu
from jax.sharding import PartitionSpec as P

MESH = pl.DeviceIdType.MESH
LIFT = 2.0**18
TINY = 1e-37
LOG2E = 1.4426950408889634
HALF = 64
ROWS = 128
NT = (((1,), (1,)), ((), ()))
TN = (((0,), (0,)), ((), ()))

Z_RIGHT, Z_LEFT = 0, 16
S_RIGHT, S_LEFT = 32, 48
T_CORE, T_Y, T_X = 64, 69, 71
G_CORE, G_Y, G_X = 73, 77, 81
N_SEM = 83
PIECES = 2


def code(v):
    w = v * LIFT
    w = w * jnp.abs(w)
    w = w * jnp.abs(w)
    return w.astype(jnp.bfloat16)


def decode(u):
    u = u.astype(jnp.float32)
    r = lax.rsqrt(lax.rsqrt(jnp.maximum(jnp.abs(u), TINY))) * (1.0 / LIFT)
    return jnp.where(u < 0.0, -r, r)


def kernel(
    x_ref, t_ref, scale_ref, bias_ref, vis_ref, txt_ref,
    xb, tb, cb, vp, gp, sl, sr, rl, rr, core_out, core_in, y_out, y_in, x_out, x_in, ss, rs, own,
):
    blk = lax.axis_index("blk")
    grp = lax.axis_index("grp")
    z, y, core = grp // 4, (grp // 2) % 2, grp % 2
    right = (blk, ((z + 1) % 8) * 4 + y * 2 + core)
    left = (blk, ((z + 7) % 8) * 4 + y * 2 + core)
    across = (blk, z * 4 + (1 - y) * 2 + core)
    sibling = (blk, z * 4 + y * 2 + (1 - core))
    flip_down = 1 - (blk % 4 + 3) // 4
    up_blk = (blk + 1) % 8
    flip_up = 1 - (up_blk % 4 + 3) // 4
    down = ((blk + 7) % 8, z * 4 + ((y + flip_down) % 2) * 2 + core)
    up = (up_blk, z * 4 + ((y + flip_up) % 2) * 2 + core)

    own_image = pltpu.make_async_copy(x_ref, xb.at[pl.ds(0, ROWS)], own.at[0])
    own_text = pltpu.make_async_copy(t_ref, tb.at[pl.ds(0, ROWS)], own.at[1])
    own_image.start()
    own_text.start()

    barrier = pltpu.get_barrier_semaphore()
    for other in (right, left, across, sibling, down, up):
        pl.semaphore_signal(barrier, inc=1, device_id=other, device_id_type=MESH)
    pl.semaphore_wait(barrier, 6)

    copies = []

    def send(k, src, dst, device):
        copy = pltpu.make_async_remote_copy(
            src_ref=src, dst_ref=dst, send_sem=ss.at[k], recv_sem=rs.at[k],
            device_id=device, device_id_type=MESH,
        )
        copy.start()
        copies.append(copy)
        return copy

    low, high = pl.ds(0, HALF), pl.ds(HALF, HALF)

    def text(h, yy, cc):
        return pl.ds(512 * h + 256 * yy + 128 * cc, 128)

    zr, zl, tc = {}, {}, {}
    step = HALF // PIECES

    def go_round(i, p):
        at = pl.ds(ROWS * i + step * p, step)
        there = pl.ds(ROWS * i + HALF + step * p, step)
        if i <= 2:
            right_start, left_start = (0, HALF) if i == 1 else (HALF, 0)
            to_right, to_left = x_ref.at[pl.ds(right_start + step * p, step)], x_ref.at[pl.ds(left_start + step * p, step)]
        else:
            to_right = xb.at[pl.ds(ROWS * (i - 2) + step * p, step)]
            to_left = xb.at[pl.ds(ROWS * (i - 2) + HALF + step * p, step)]
        zr[i, p] = send(Z_RIGHT + PIECES * i + p, to_right, xb.at[at], right)
        zl[i, p] = send(Z_LEFT + PIECES * i + p, to_left, xb.at[there], left)

    for p in range(PIECES):
        go_round(1, p)
    ty0 = send(T_Y, t_ref, tb.at[text(0, 1, 0)], across)
    tx = send(T_X, t_ref, tb.at[text(1, 0, 0)], up)
    tc[0, 0] = send(T_CORE, t_ref, tb.at[text(0, 0, 1)], sibling)
    for p in range(PIECES):
        zr[1, p].wait_send()
        zl[1, p].wait_send()
        go_round(2, p)

    scale = scale_ref[0]
    slope = scale * (-LOG2E)
    shift = bias_ref[0] * LOG2E

    def arrive(i):
        for p in range(PIECES):
            zr[i, p].wait_recv()
            zl[i, p].wait_recv()
            if i + 2 <= 7:
                go_round(i + 2, p)

    def coefficients(start, rows, first, last):
        x = xb[start : start + rows, :]

        def tile(n, carry):
            texts = pl.ds(pl.multiple_of(n * 256, 256), 256)
            dots = lax.dot_general(tb[texts, :], x, NT, preferred_element_type=jnp.float32)
            away = 1.0 + jnp.exp2(jnp.minimum(dots * slope - shift, 126.0))
            c = pl.reciprocal(away, approx=True)
            c = c * (2.0 - away * c)
            if start == 0 and first == 0:
                row = lax.broadcasted_iota(jnp.int32, c.shape, 0) + n * 256
                col = lax.broadcasted_iota(jnp.int32, c.shape, 1)
                c = jnp.where((row == col) & (row < ROWS), c - 1.0, c)
            cb[texts, start : start + rows] = c.astype(jnp.bfloat16)
            return carry

        lax.fori_loop(first, last, tile, 0)

    def image_terms(start, rows):
        vp[start : start + rows, :] = lax.dot_general(
            cb[:, start : start + rows], tb[...], TN, preferred_element_type=jnp.float32
        )

    def text_terms(quarter):
        texts = pl.ds(256 * quarter, 256)
        gp[texts, :] = jnp.dot(cb[texts, :], xb[...], preferred_element_type=jnp.float32)

    vl, vr = {}, {}

    def pass_on(i):
        for p in range(PIECES):
            part = pl.ds(p * HALF // PIECES, HALF // PIECES)
            for way, (sent, out, came, to, k) in enumerate(
                ((vl, sl, rl, left, S_LEFT), (vr, sr, rr, right, S_RIGHT))
            ):
                total = vp[pl.ds(ROWS * i + HALF * way + p * HALF // PIECES, HALF // PIECES), :]
                if i <= 5:
                    sent[i + 2, p].wait_recv()
                    total = total + decode(came[i + 2, part, :])
                out[i, part, :] = code(total)
                sent[i, p] = send(k + PIECES * i + p, out.at[i, part], came.at[i, part], to)

    def code_rows(dst, src, src_start, count):
        def some(k, carry):
            at = pl.multiple_of(k * 64, 64)
            dst[pl.ds(at, 64), :] = code(src[pl.ds(src_start + at, 64), :])
            return carry

        lax.fori_loop(0, count // 64, some, 0)

    gc = {}

    def text_to_sibling(h, yy):
        code_rows(core_out.at[h, yy], gp, 512 * h + 256 * yy + 128, 128)
        gc[h, yy] = send(G_CORE + 2 * h + yy, core_out.at[h, yy], core_in.at[h, yy], sibling)

    gy = {}

    def text_across(h):
        gc[h, 1].wait_recv()
        for k in range(2):
            at = pl.ds(64 * k, 64)
            y_out[h, at, :] = code(gp[pl.ds(512 * h + 256 + 64 * k, 64), :] + decode(core_in[h, 1, at, :]))
            gy[h, k] = send(G_Y + 2 * h + k, y_out.at[h, at], y_in.at[h, at], across)

    def text_sum(h, k):
        at = pl.ds(64 * k, 64)
        if k == 0:
            gc[h, 0].wait_recv()
        gy[h, k].wait_recv()
        near = gp[pl.ds(512 * h + 64 * k, 64), :]
        return near + decode(core_in[h, 0, at, :]) + decode(y_in[h, at, :])

    own_text.wait()
    own_image.wait()
    arrive(1)
    tc[0, 0].wait_recv()
    coefficients(0, 256, 0, 1)
    ty0.wait_recv()
    far_low, far_high = pl.ds(768, HALF), pl.ds(768 + HALF, HALF)
    tx1 = send(T_X + 1, tb.at[pl.ds(256 + HALF, HALF)], tb.at[far_high], up)
    tc[0, 1] = send(T_CORE + 1, tb.at[text(0, 1, 0)], tb.at[text(0, 1, 1)], sibling)
    tx.wait_recv()
    ty1 = send(T_Y + 1, tb.at[pl.ds(512, HALF)], tb.at[far_low], across)
    tc[1, 0] = send(T_CORE + 2, tb.at[text(1, 0, 0)], tb.at[text(1, 0, 1)], sibling)
    arrive(2)
    tc[0, 1].wait_recv()
    tc[1, 0].wait_recv()
    coefficients(0, 256, 1, 3)
    arrive(3)
    ty1.wait_recv()
    tc[1, 1] = send(T_CORE + 3, tb.at[far_low], tb.at[pl.ds(896, HALF)], sibling)
    tx1.wait_recv()
    tc[1, 2] = send(T_CORE + 4, tb.at[far_high], tb.at[pl.ds(896 + HALF, HALF)], sibling)
    coefficients(256, 256, 0, 3)
    tc[1, 1].wait_recv()
    tc[1, 2].wait_recv()
    arrive(4)
    coefficients(256, 256, 3, 4)
    coefficients(0, 256, 3, 4)
    image_terms(256, 256)
    arrive(5)
    coefficients(512, 256, 0, 4)
    image_terms(512, 256)
    arrive(6)
    coefficients(768, 128, 0, 4)
    image_terms(768, 128)
    pass_on(6)
    arrive(7)
    coefficients(896, 128, 0, 4)
    image_terms(896, 128)
    pass_on(7)
    text_terms(3)
    text_to_sibling(1, 1)
    pass_on(4)
    text_across(1)
    text_terms(2)
    text_to_sibling(1, 0)
    pass_on(5)
    text_terms(1)
    text_to_sibling(0, 1)
    gx = {}

    def text_down(k):
        at = pl.ds(64 * k, 64)
        x_out[at, :] = code(text_sum(1, k))
        gx[k] = send(G_X + k, x_out.at[at], x_in.at[at], down)

    text_down(0)
    pass_on(2)
    text_across(0)
    text_down(1)
    text_terms(0)
    text_to_sibling(0, 0)
    pass_on(3)
    image_terms(0, 256)
    pass_on(1)
    for p in range(PIECES):
        vl[2, p].wait_recv()
        vr[2, p].wait_recv()
    vp[low, :] = vp[low, :] + decode(rr[2])
    vp[high, :] = vp[high, :] + decode(rl[2])
    for k in range(2):
        gp[pl.ds(64 * k, 64), :] = text_sum(0, k)
    for k in range(2):
        at = pl.ds(64 * k, 64)
        gx[k].wait_recv()
        txt_ref[at, :] = (gp[at, :] + decode(x_in[at, :]))
    for p in range(PIECES):
        vl[1, p].wait_recv()
        vr[1, p].wait_recv()
    vis_ref[low, :] = (vp[low, :] + decode(rl[1]))
    vis_ref[high, :] = (vp[high, :] + decode(rr[1]))
    for copy in copies:
        if not any(copy is zr[1, p] or copy is zl[1, p] for p in range(PIECES)):
            copy.wait_send()


def per_device(images, texts, scale, bias):
    rows, width = images.shape
    bf16, f32 = jnp.bfloat16, jnp.float32
    out = jax.ShapeDtypeStruct((rows, width), f32)
    vmem = pl.BlockSpec(memory_space=pltpu.VMEM)
    hbm = pl.BlockSpec(memory_space=pltpu.HBM)
    smem = pl.BlockSpec(memory_space=pltpu.SMEM)
    visual, textual = pl.pallas_call(
        kernel,
        out_shape=(out, out),
        in_specs=[hbm, hbm, smem, smem],
        out_specs=(vmem, vmem),
        scratch_shapes=[
            pltpu.VMEM((1024, width), bf16),
            pltpu.VMEM((1024, width), bf16),
            pltpu.VMEM((1024, 1024), bf16),
            pltpu.VMEM((1024, width), f32),
            pltpu.VMEM((1024, width), f32),
            pltpu.VMEM((8, HALF, width), bf16),
            pltpu.VMEM((8, HALF, width), bf16),
            pltpu.VMEM((8, HALF, width), bf16),
            pltpu.VMEM((8, HALF, width), bf16),
            pltpu.VMEM((2, 2, ROWS, width), bf16),
            pltpu.VMEM((2, 2, ROWS, width), bf16),
            pltpu.VMEM((2, ROWS, width), bf16),
            pltpu.VMEM((2, ROWS, width), bf16),
            pltpu.VMEM((ROWS, width), bf16),
            pltpu.VMEM((ROWS, width), bf16),
            pltpu.SemaphoreType.DMA((N_SEM,)),
            pltpu.SemaphoreType.DMA((N_SEM,)),
            pltpu.SemaphoreType.DMA((2,)),
        ],
        compiler_params=pltpu.CompilerParams(
            collective_id=0, has_side_effects=True, vmem_limit_bytes=48 * 1024 * 1024
        ),
        cost_estimate=pl.CostEstimate(
            flops=6 * 1024 * 1024 * width, bytes_accessed=12 * rows * width, transcendentals=2 * 1024 * 1024
        ),
    )(pltpu.with_memory_space_constraint(images, pltpu.HBM), pltpu.with_memory_space_constraint(texts, pltpu.HBM), scale, bias)
    return scale[0] * visual, scale[0] * textual


def solution(mesh):
    spec = P(("blk", "grp"), None)
    return jax.shard_map(
        per_device,
        mesh=mesh,
        in_specs=(spec, spec, P(), P()),
        out_specs=(spec, spec),
        check_vma=False,
    )
```

```python
import functools

import jax
import jax.numpy as jnp
from jax import lax
from jax.experimental import pallas as pl
from jax.experimental.pallas import tpu as pltpu
from jax.sharding import PartitionSpec as P

MESH = pl.DeviceIdType.MESH
LIFT = 2.0**18
TINY = 1e-37
LOG2E = 1.4426950408889634
HALF = 64
ROWS = 128
NT = (((1,), (1,)), ((), ()))
TN = (((0,), (0,)), ((), ()))

Z_RIGHT, Z_LEFT = 0, 16
S_RIGHT, S_LEFT = 32, 48
T_CORE, T_Y, T_X = 64, 69, 71
G_CORE, G_Y, G_X = 73, 77, 81
N_SEM = 83
PIECES = 2


def code(v):
    w = v * LIFT
    w = w * jnp.abs(w)
    w = w * jnp.abs(w)
    return w.astype(jnp.bfloat16)


def decode(u):
    u = u.astype(jnp.float32)
    r = lax.rsqrt(lax.rsqrt(jnp.maximum(jnp.abs(u), TINY))) * (1.0 / LIFT)
    return jnp.where(u < 0.0, -r, r)


def kernel(
    x_ref, t_ref, scale_ref, bias_ref, vis_ref, txt_ref,
    xb, tb, cb, db, vp, gp, sl, sr, rl, rr, core_out, core_in, y_out, y_in, x_out, x_in, ss, rs, own,
):
    blk = lax.axis_index("blk")
    grp = lax.axis_index("grp")
    z, y, core = grp // 4, (grp // 2) % 2, grp % 2
    right = (blk, ((z + 1) % 8) * 4 + y * 2 + core)
    left = (blk, ((z + 7) % 8) * 4 + y * 2 + core)
    across = (blk, z * 4 + (1 - y) * 2 + core)
    sibling = (blk, z * 4 + y * 2 + (1 - core))
    flip_down = 1 - (blk % 4 + 3) // 4
    up_blk = (blk + 1) % 8
    flip_up = 1 - (up_blk % 4 + 3) // 4
    down = ((blk + 7) % 8, z * 4 + ((y + flip_down) % 2) * 2 + core)
    up = (up_blk, z * 4 + ((y + flip_up) % 2) * 2 + core)

    own_image = pltpu.make_async_copy(x_ref, xb.at[pl.ds(0, ROWS)], own.at[0])
    own_text = pltpu.make_async_copy(t_ref, tb.at[pl.ds(0, ROWS)], own.at[1])
    own_image.start()
    own_text.start()

    barrier = pltpu.get_barrier_semaphore()
    for other in (right, left, across, sibling, down):
        pl.semaphore_signal(barrier, inc=1, device_id=other, device_id_type=MESH)
    pl.semaphore_wait(barrier, 5)

    copies = []

    def send(k, src, dst, device):
        copy = pltpu.make_async_remote_copy(
            src_ref=src, dst_ref=dst, send_sem=ss.at[k], recv_sem=rs.at[k],
            device_id=device, device_id_type=MESH,
        )
        copy.start()
        copies.append(copy)
        return copy

    low, high = pl.ds(0, HALF), pl.ds(HALF, HALF)

    def text(h, yy, cc):
        return pl.ds(512 * h + 256 * yy + 128 * cc, 128)

    zr, zl, tc = {}, {}, {}
    step = HALF // PIECES

    def go_round(i, p):
        at = pl.ds(ROWS * i + step * p, step)
        there = pl.ds(ROWS * i + HALF + step * p, step)
        if i <= 2:
            right_start, left_start = (0, HALF) if i == 1 else (HALF, 0)
            to_right, to_left = x_ref.at[pl.ds(right_start + step * p, step)], x_ref.at[pl.ds(left_start + step * p, step)]
        else:
            to_right = xb.at[pl.ds(ROWS * (i - 2) + step * p, step)]
            to_left = xb.at[pl.ds(ROWS * (i - 2) + HALF + step * p, step)]
        zr[i, p] = send(Z_RIGHT + PIECES * i + p, to_right, xb.at[at], right)
        zl[i, p] = send(Z_LEFT + PIECES * i + p, to_left, xb.at[there], left)

    for p in range(PIECES):
        go_round(1, p)
    ty0 = send(T_Y, t_ref, tb.at[text(0, 1, 0)], across)
    tx = send(T_X, t_ref, tb.at[text(1, 0, 0)], up)
    tc[0, 0] = send(T_CORE, t_ref, tb.at[text(0, 0, 1)], sibling)
    for p in range(PIECES):
        zr[1, p].wait_send()
        zl[1, p].wait_send()
        go_round(2, p)

    scale = scale_ref[0]
    slope = scale * (-LOG2E)
    shift = bias_ref[0] * LOG2E

    def arrive(i):
        for p in range(PIECES):
            zr[i, p].wait_recv()
            zl[i, p].wait_recv()
            if i + 2 <= 7:
                go_round(i + 2, p)

    def coefficients(start, rows, first, last):
        some = pl.ds(256 * first, 256 * (last - first))
        db[some, 0:rows] = lax.dot_general(
            tb[some, :], xb[start : start + rows, :], NT, preferred_element_type=jnp.float32
        )

        def tile(n, carry):
            texts = pl.ds(pl.multiple_of(n * 256, 256), 256)
            away = 1.0 + jnp.exp2(jnp.minimum(db[texts, 0:rows] * slope - shift, 126.0))
            c = pl.reciprocal(away, approx=True)
            c = c * (2.0 - away * c)
            if start == 0 and first == 0:
                row = lax.broadcasted_iota(jnp.int32, c.shape, 0) + n * 256
                col = lax.broadcasted_iota(jnp.int32, c.shape, 1)
                c = jnp.where((row == col) & (row < ROWS), c - 1.0, c)
            cb[texts, start : start + rows] = c.astype(jnp.bfloat16)
            return carry

        lax.fori_loop(first, last, tile, 0)

    def image_terms(start, rows):
        vp[start : start + rows, :] = lax.dot_general(
            cb[:, start : start + rows], tb[...], TN, preferred_element_type=jnp.float32
        )

    def text_terms(quarter):
        texts = pl.ds(256 * quarter, 256)
        gp[texts, :] = jnp.dot(cb[texts, :], xb[...], preferred_element_type=jnp.float32)

    vl, vr = {}, {}

    def pass_on(i):
        for p in range(PIECES):
            part = pl.ds(p * HALF // PIECES, HALF // PIECES)
            for way, (sent, out, came, to, k) in enumerate(
                ((vl, sl, rl, left, S_LEFT), (vr, sr, rr, right, S_RIGHT))
            ):
                total = vp[pl.ds(ROWS * i + HALF * way + p * HALF // PIECES, HALF // PIECES), :]
                if i <= 5:
                    sent[i + 2, p].wait_recv()
                    total = total + decode(came[i + 2, part, :])
                out[i, part, :] = code(total)
                sent[i, p] = send(k + PIECES * i + p, out.at[i, part], came.at[i, part], to)

    def code_rows(dst, src, src_start, count):
        def some(k, carry):
            at = pl.multiple_of(k * 64, 64)
            dst[pl.ds(at, 64), :] = code(src[pl.ds(src_start + at, 64), :])
            return carry

        lax.fori_loop(0, count // 64, some, 0)

    gc = {}

    def text_to_sibling(h, yy):
        code_rows(core_out.at[h, yy], gp, 512 * h + 256 * yy + 128, 128)
        gc[h, yy] = send(G_CORE + 2 * h + yy, core_out.at[h, yy], core_in.at[h, yy], sibling)

    gy = {}

    def text_across(h):
        gc[h, 1].wait_recv()
        for k in range(2):
            at = pl.ds(64 * k, 64)
            y_out[h, at, :] = code(gp[pl.ds(512 * h + 256 + 64 * k, 64), :] + decode(core_in[h, 1, at, :]))
            gy[h, k] = send(G_Y + 2 * h + k, y_out.at[h, at], y_in.at[h, at], across)

    def text_sum(h, k):
        at = pl.ds(64 * k, 64)
        if k == 0:
            gc[h, 0].wait_recv()
        gy[h, k].wait_recv()
        near = gp[pl.ds(512 * h + 64 * k, 64), :]
        return near + decode(core_in[h, 0, at, :]) + decode(y_in[h, at, :])

    own_text.wait()
    own_image.wait()
    arrive(1)
    tc[0, 0].wait_recv()
    coefficients(0, 256, 0, 1)
    ty0.wait_recv()
    far_low, far_high = pl.ds(768, HALF), pl.ds(768 + HALF, HALF)
    tx1 = send(T_X + 1, tb.at[pl.ds(256 + HALF, HALF)], tb.at[far_high], up)
    tc[0, 1] = send(T_CORE + 1, tb.at[text(0, 1, 0)], tb.at[text(0, 1, 1)], sibling)
    tx.wait_recv()
    ty1 = send(T_Y + 1, tb.at[pl.ds(512, HALF)], tb.at[far_low], across)
    tc[1, 0] = send(T_CORE + 2, tb.at[text(1, 0, 0)], tb.at[text(1, 0, 1)], sibling)
    arrive(2)
    tc[0, 1].wait_recv()
    tc[1, 0].wait_recv()
    coefficients(0, 256, 1, 3)
    arrive(3)
    ty1.wait_recv()
    tc[1, 1] = send(T_CORE + 3, tb.at[far_low], tb.at[pl.ds(896, HALF)], sibling)
    tx1.wait_recv()
    tc[1, 2] = send(T_CORE + 4, tb.at[far_high], tb.at[pl.ds(896 + HALF, HALF)], sibling)
    coefficients(256, 256, 0, 3)
    tc[1, 1].wait_recv()
    tc[1, 2].wait_recv()
    arrive(4)
    coefficients(256, 256, 3, 4)
    coefficients(0, 256, 3, 4)
    image_terms(256, 256)
    arrive(5)
    coefficients(512, 256, 0, 4)
    image_terms(512, 256)
    arrive(6)
    coefficients(768, 128, 0, 4)
    image_terms(768, 128)
    pass_on(6)
    arrive(7)
    coefficients(896, 128, 0, 4)
    image_terms(896, 128)
    pass_on(7)
    text_terms(3)
    text_to_sibling(1, 1)
    pass_on(4)
    text_across(1)
    text_terms(2)
    text_to_sibling(1, 0)
    pass_on(5)
    text_terms(1)
    text_to_sibling(0, 1)
    gx = {}

    def text_down(k):
        at = pl.ds(64 * k, 64)
        x_out[at, :] = code(text_sum(1, k))
        gx[k] = send(G_X + k, x_out.at[at], x_in.at[at], down)

    text_down(0)
    pass_on(2)
    text_across(0)
    text_down(1)
    text_terms(0)
    text_to_sibling(0, 0)
    pass_on(3)
    image_terms(0, 256)
    pass_on(1)
    for p in range(PIECES):
        vl[2, p].wait_recv()
        vr[2, p].wait_recv()
    vp[low, :] = vp[low, :] + decode(rr[2])
    vp[high, :] = vp[high, :] + decode(rl[2])
    for k in range(2):
        gp[pl.ds(64 * k, 64), :] = text_sum(0, k)
    for k in range(2):
        at = pl.ds(64 * k, 64)
        gx[k].wait_recv()
        txt_ref[at, :] = (gp[at, :] + decode(x_in[at, :]))
    for p in range(PIECES):
        vl[1, p].wait_recv()
        vr[1, p].wait_recv()
    vis_ref[low, :] = (vp[low, :] + decode(rl[1]))
    vis_ref[high, :] = (vp[high, :] + decode(rr[1]))
    for copy in copies:
        if not any(copy is zr[1, p] or copy is zl[1, p] for p in range(PIECES)):
            copy.wait_send()


def per_device(images, texts, scale, bias):
    rows, width = images.shape
    bf16, f32 = jnp.bfloat16, jnp.float32
    out = jax.ShapeDtypeStruct((rows, width), f32)
    vmem = pl.BlockSpec(memory_space=pltpu.VMEM)
    hbm = pl.BlockSpec(memory_space=pltpu.HBM)
    smem = pl.BlockSpec(memory_space=pltpu.SMEM)
    visual, textual = pl.pallas_call(
        kernel,
        out_shape=(out, out),
        in_specs=[hbm, hbm, smem, smem],
        out_specs=(vmem, vmem),
        scratch_shapes=[
            pltpu.VMEM((1024, width), bf16),
            pltpu.VMEM((1024, width), bf16),
            pltpu.VMEM((1024, 1024), bf16),
            pltpu.VMEM((1024, 256), f32),
            pltpu.VMEM((1024, width), f32),
            pltpu.VMEM((1024, width), f32),
            pltpu.VMEM((8, HALF, width), bf16),
            pltpu.VMEM((8, HALF, width), bf16),
            pltpu.VMEM((8, HALF, width), bf16),
            pltpu.VMEM((8, HALF, width), bf16),
            pltpu.VMEM((2, 2, ROWS, width), bf16),
            pltpu.VMEM((2, 2, ROWS, width), bf16),
            pltpu.VMEM((2, ROWS, width), bf16),
            pltpu.VMEM((2, ROWS, width), bf16),
            pltpu.VMEM((ROWS, width), bf16),
            pltpu.VMEM((ROWS, width), bf16),
            pltpu.SemaphoreType.DMA((N_SEM,)),
            pltpu.SemaphoreType.DMA((N_SEM,)),
            pltpu.SemaphoreType.DMA((2,)),
        ],
        compiler_params=pltpu.CompilerParams(
            collective_id=0, has_side_effects=True, vmem_limit_bytes=48 * 1024 * 1024
        ),
        cost_estimate=pl.CostEstimate(
            flops=6 * 1024 * 1024 * width, bytes_accessed=12 * rows * width, transcendentals=2 * 1024 * 1024
        ),
    )(pltpu.with_memory_space_constraint(images, pltpu.HBM), pltpu.with_memory_space_constraint(texts, pltpu.HBM), scale, bias)
    return scale[0] * visual, scale[0] * textual


def solution(mesh):
    spec = P(("blk", "grp"), None)
    return jax.shard_map(
        per_device,
        mesh=mesh,
        in_specs=(spec, spec, P(), P()),
        out_specs=(spec, spec),
        check_vma=False,
    )
```

```python
import functools

import jax
import jax.numpy as jnp
from jax import lax
from jax.experimental import pallas as pl
from jax.experimental.pallas import tpu as pltpu
from jax.sharding import PartitionSpec as P

MESH = pl.DeviceIdType.MESH
LIFT = 2.0**18
TINY = 1e-37
LOG2E = 1.4426950408889634
HALF = 64
ROWS = 128
NT = (((1,), (1,)), ((), ()))
TN = (((0,), (0,)), ((), ()))

Z_RIGHT, Z_LEFT = 0, 16
S_RIGHT, S_LEFT = 32, 48
T_CORE, T_Y, T_X = 64, 69, 71
G_CORE, G_Y, G_X = 73, 77, 81
N_SEM = 84
PIECES = 2


def code(v):
    w = v * LIFT
    w = w * jnp.abs(w)
    w = w * jnp.abs(w)
    return w.astype(jnp.bfloat16)


def decode(u):
    u = u.astype(jnp.float32)
    r = lax.rsqrt(lax.rsqrt(jnp.maximum(jnp.abs(u), TINY))) * (1.0 / LIFT)
    return jnp.where(u < 0.0, -r, r)


def kernel(
    x_ref, t_ref, scale_ref, bias_ref, vis_ref, txt_ref,
    xb, tb, cb, db, vp, gp, sl, sr, rl, rr, core_in, y_out, y_in, x_out, x_in, ss, rs, own,
):
    blk = lax.axis_index("blk")
    grp = lax.axis_index("grp")
    z, y, core = grp // 4, (grp // 2) % 2, grp % 2
    right = (blk, ((z + 1) % 8) * 4 + y * 2 + core)
    left = (blk, ((z + 7) % 8) * 4 + y * 2 + core)
    across = (blk, z * 4 + (1 - y) * 2 + core)
    sibling = (blk, z * 4 + y * 2 + (1 - core))
    flip_down = 1 - (blk % 4 + 3) // 4
    up_blk = (blk + 1) % 8
    flip_up = 1 - (up_blk % 4 + 3) // 4
    down = ((blk + 7) % 8, z * 4 + ((y + flip_down) % 2) * 2 + core)
    up = (up_blk, z * 4 + ((y + flip_up) % 2) * 2 + core)

    own_image = pltpu.make_async_copy(x_ref, xb.at[pl.ds(0, ROWS)], own.at[0])
    own_text = pltpu.make_async_copy(t_ref, tb.at[pl.ds(0, ROWS)], own.at[1])
    own_image.start()
    own_text.start()

    barrier = pltpu.get_barrier_semaphore()
    for other in (right, left, across, sibling, down):
        pl.semaphore_signal(barrier, inc=1, device_id=other, device_id_type=MESH)
    pl.semaphore_wait(barrier, 5)

    copies = []

    def send(k, src, dst, device):
        copy = pltpu.make_async_remote_copy(
            src_ref=src, dst_ref=dst, send_sem=ss.at[k], recv_sem=rs.at[k],
            device_id=device, device_id_type=MESH,
        )
        copy.start()
        copies.append(copy)
        return copy

    low, high = pl.ds(0, HALF), pl.ds(HALF, HALF)

    def text(h, yy, cc):
        return pl.ds(512 * h + 256 * yy + 128 * cc, 128)

    zr, zl, tc = {}, {}, {}
    step = HALF // PIECES

    def go_round(i, p):
        at = pl.ds(ROWS * i + step * p, step)
        there = pl.ds(ROWS * i + HALF + step * p, step)
        if i <= 2:
            right_start, left_start = (0, HALF) if i == 1 else (HALF, 0)
            to_right, to_left = x_ref.at[pl.ds(right_start + step * p, step)], x_ref.at[pl.ds(left_start + step * p, step)]
        else:
            to_right = xb.at[pl.ds(ROWS * (i - 2) + step * p, step)]
            to_left = xb.at[pl.ds(ROWS * (i - 2) + HALF + step * p, step)]
        zr[i, p] = send(Z_RIGHT + PIECES * i + p, to_right, xb.at[at], right)
        zl[i, p] = send(Z_LEFT + PIECES * i + p, to_left, xb.at[there], left)

    for p in range(PIECES):
        go_round(1, p)
    ty0 = send(T_Y, t_ref, tb.at[text(0, 1, 0)], across)
    tx = send(T_X, t_ref, tb.at[text(1, 0, 0)], up)
    tc[0, 0] = send(T_CORE, t_ref, tb.at[text(0, 0, 1)], sibling)
    for p in range(PIECES):
        zr[1, p].wait_send()
        zl[1, p].wait_send()
        go_round(2, p)

    scale = scale_ref[0]
    slope = scale * (-LOG2E)
    shift = bias_ref[0] * LOG2E

    def arrive(i):
        for p in range(PIECES):
            zr[i, p].wait_recv()
            zl[i, p].wait_recv()
            if i + 2 <= 7:
                go_round(i + 2, p)

    def coefficients(start, rows, first, last):
        some = pl.ds(256 * first, 256 * (last - first))
        db[some, 0:rows] = lax.dot_general(
            tb[some, :], xb[start : start + rows, :], NT, preferred_element_type=jnp.float32
        )

        def tile(n, carry):
            texts = pl.ds(pl.multiple_of(n * 256, 256), 256)
            away = 1.0 + jnp.exp2(jnp.minimum(db[texts, 0:rows] * slope - shift, 126.0))
            c = pl.reciprocal(away, approx=True)
            c = c * (2.0 - away * c)
            if start == 0 and first == 0:
                row = lax.broadcasted_iota(jnp.int32, c.shape, 0) + n * 256
                col = lax.broadcasted_iota(jnp.int32, c.shape, 1)
                c = jnp.where((row == col) & (row < ROWS), c - 1.0, c)
            cb[texts, start : start + rows] = c.astype(jnp.bfloat16)
            return carry

        lax.fori_loop(first, last, tile, 0)

    def image_terms(start, rows):
        vp[start : start + rows, :] = lax.dot_general(
            cb[:, start : start + rows], tb[...], TN, preferred_element_type=jnp.float32
        )

    def text_terms(quarter):
        texts = pl.ds(256 * quarter, 256)
        gp[texts, :] = jnp.dot(cb[texts, :], xb[...], preferred_element_type=jnp.float32)

    vl, vr = {}, {}

    def pass_on(i):
        for p in range(PIECES):
            part = pl.ds(p * HALF // PIECES, HALF // PIECES)
            for way, (sent, out, came, to, k) in enumerate(
                ((vl, sl, rl, left, S_LEFT), (vr, sr, rr, right, S_RIGHT))
            ):
                total = vp[pl.ds(ROWS * i + HALF * way + p * HALF // PIECES, HALF // PIECES), :]
                if i <= 5:
                    sent[i + 2, p].wait_recv()
                    total = total + decode(came[i + 2, part, :])
                out[i, part, :] = code(total)
                sent[i, p] = send(k + PIECES * i + p, out.at[i, part], came.at[i, part], to)

    gc = {}

    def text_to_sibling(h, yy):
        src = gp.at[pl.ds(512 * h + 256 * yy + 128, 128)]
        gc[h, yy] = send(G_CORE + 2 * h + yy, src, core_in.at[h, yy], sibling)

    gy, gx = {}, {}

    def near_pair(h, yy, k):
        at = 64 * k
        ready(h, yy)
        return gp[pl.ds(512 * h + 256 * yy + at, 64), :] + core_in[h, yy, pl.ds(at, 64), :]

    waited = set()

    def ready(h, yy):
        if (h, yy) not in waited:
            waited.add((h, yy))
            gc[h, yy].wait_recv()

    def far_lower_out():
        y_out[1, low, :] = code(near_pair(1, 1, 0))
        gy[1, 0] = send(G_Y + 2, y_out.at[1, low], y_in.at[1, low], across)
        y_out[1, high, :] = code(near_pair(1, 1, 1))
        gx[2] = send(G_X + 2, y_out.at[1, high], y_in.at[1, high], down)

    def near_lower_out(k):
        at = pl.ds(64 * k, 64)
        total = near_pair(1, 0, k)
        if k == 0:
            gy[1, 0].wait_recv()
            total = total + decode(y_in[1, low, :])
        x_out[at, :] = code(total)
        gx[k] = send(G_X + k, x_out.at[at], x_in.at[at], down)

    def far_own_out(k):
        at = pl.ds(64 * k, 64)
        total = near_pair(0, 1, k)
        if k == 1:
            gx[2].wait_recv()
            total = total + decode(y_in[1, high, :])
        y_out[0, at, :] = code(total)
        gy[0, k] = send(G_Y + k, y_out.at[0, at], y_in.at[0, at], across)

    def near_own_sum(k):
        at = pl.ds(64 * k, 64)
        total = near_pair(0, 0, k)
        gy[0, k].wait_recv()
        total = total + decode(y_in[0, at, :])
        gx[k].wait_recv()
        txt_ref[at, :] = total + decode(x_in[at, :])

    own_text.wait()
    own_image.wait()
    arrive(1)
    tc[0, 0].wait_recv()
    coefficients(0, 256, 0, 1)
    arrive(2)
    ty0.wait_recv()
    far_low, far_high = pl.ds(768, HALF), pl.ds(768 + HALF, HALF)
    tx1 = send(T_X + 1, tb.at[pl.ds(256 + HALF, HALF)], tb.at[far_high], up)
    tc[0, 1] = send(T_CORE + 1, tb.at[text(0, 1, 0)], tb.at[text(0, 1, 1)], sibling)
    tx.wait_recv()
    ty1 = send(T_Y + 1, tb.at[pl.ds(512, HALF)], tb.at[far_low], across)
    tc[1, 0] = send(T_CORE + 2, tb.at[text(1, 0, 0)], tb.at[text(1, 0, 1)], sibling)
    tc[0, 1].wait_recv()
    tc[1, 0].wait_recv()
    coefficients(0, 256, 1, 3)
    arrive(3)
    ty1.wait_recv()
    tc[1, 1] = send(T_CORE + 3, tb.at[far_low], tb.at[pl.ds(896, HALF)], sibling)
    tx1.wait_recv()
    tc[1, 2] = send(T_CORE + 4, tb.at[far_high], tb.at[pl.ds(896 + HALF, HALF)], sibling)
    coefficients(256, 256, 0, 3)
    tc[1, 1].wait_recv()
    tc[1, 2].wait_recv()
    arrive(4)
    coefficients(256, 256, 3, 4)
    coefficients(0, 256, 3, 4)
    image_terms(256, 256)
    arrive(5)
    coefficients(512, 256, 0, 4)
    arrive(6)
    coefficients(768, 128, 0, 4)
    image_terms(768, 128)
    pass_on(6)
    arrive(7)
    coefficients(896, 128, 0, 4)
    image_terms(896, 128)
    pass_on(7)
    image_terms(512, 256)
    pass_on(4)
    text_terms(3)
    text_to_sibling(1, 1)
    text_terms(2)
    text_to_sibling(1, 0)
    pass_on(5)
    far_lower_out()
    near_lower_out(1)
    text_terms(1)
    text_to_sibling(0, 1)
    pass_on(2)
    text_terms(0)
    text_to_sibling(0, 0)
    far_own_out(0)
    far_own_out(1)
    near_lower_out(0)
    pass_on(3)
    image_terms(0, 256)
    pass_on(1)
    for p in range(PIECES):
        vl[2, p].wait_recv()
        vr[2, p].wait_recv()
    vp[low, :] = vp[low, :] + decode(rr[2])
    vp[high, :] = vp[high, :] + decode(rl[2])
    for k in range(2):
        near_own_sum(k)
    for p in range(PIECES):
        vl[1, p].wait_recv()
        vr[1, p].wait_recv()
    vis_ref[low, :] = (vp[low, :] + decode(rl[1]))
    vis_ref[high, :] = (vp[high, :] + decode(rr[1]))
    for copy in copies:
        if not any(copy is zr[1, p] or copy is zl[1, p] for p in range(PIECES)):
            copy.wait_send()


def per_device(images, texts, scale, bias):
    rows, width = images.shape
    bf16, f32 = jnp.bfloat16, jnp.float32
    out = jax.ShapeDtypeStruct((rows, width), f32)
    vmem = pl.BlockSpec(memory_space=pltpu.VMEM)
    hbm = pl.BlockSpec(memory_space=pltpu.HBM)
    smem = pl.BlockSpec(memory_space=pltpu.SMEM)
    visual, textual = pl.pallas_call(
        kernel,
        out_shape=(out, out),
        in_specs=[hbm, hbm, smem, smem],
        out_specs=(vmem, vmem),
        scratch_shapes=[
            pltpu.VMEM((1024, width), bf16),
            pltpu.VMEM((1024, width), bf16),
            pltpu.VMEM((1024, 1024), bf16),
            pltpu.VMEM((1024, 256), f32),
            pltpu.VMEM((1024, width), f32),
            pltpu.VMEM((1024, width), f32),
            pltpu.VMEM((8, HALF, width), bf16),
            pltpu.VMEM((8, HALF, width), bf16),
            pltpu.VMEM((8, HALF, width), bf16),
            pltpu.VMEM((8, HALF, width), bf16),
            pltpu.VMEM((2, 2, ROWS, width), f32),
            pltpu.VMEM((2, ROWS, width), bf16),
            pltpu.VMEM((2, ROWS, width), bf16),
            pltpu.VMEM((ROWS, width), bf16),
            pltpu.VMEM((ROWS, width), bf16),
            pltpu.SemaphoreType.DMA((N_SEM,)),
            pltpu.SemaphoreType.DMA((N_SEM,)),
            pltpu.SemaphoreType.DMA((2,)),
        ],
        compiler_params=pltpu.CompilerParams(
            collective_id=0, has_side_effects=True, vmem_limit_bytes=48 * 1024 * 1024
        ),
        cost_estimate=pl.CostEstimate(
            flops=6 * 1024 * 1024 * width, bytes_accessed=12 * rows * width, transcendentals=2 * 1024 * 1024
        ),
    )(pltpu.with_memory_space_constraint(images, pltpu.HBM), pltpu.with_memory_space_constraint(texts, pltpu.HBM), scale, bias)
    return scale[0] * visual, scale[0] * textual


def solution(mesh):
    spec = P(("blk", "grp"), None)
    return jax.shard_map(
        per_device,
        mesh=mesh,
        in_specs=(spec, spec, P(), P()),
        out_specs=(spec, spec),
        check_vma=False,
    )
```

```python
import functools

import jax
import jax.numpy as jnp
from jax import lax
from jax.experimental import pallas as pl
from jax.experimental.pallas import tpu as pltpu
from jax.sharding import PartitionSpec as P

MESH = pl.DeviceIdType.MESH
LIFT = 2.0**18
TINY = 1e-37
LOG2E = 1.4426950408889634
HALF = 64
ROWS = 128
NT = (((1,), (1,)), ((), ()))
TN = (((0,), (0,)), ((), ()))

Z_RIGHT, Z_LEFT = 0, 16
S_RIGHT, S_LEFT = 32, 48
T_CORE, T_Y, T_X = 64, 69, 71
G_CORE, G_Y, G_X = 73, 77, 81
N_SEM = 83
PIECES = 2


def code(v):
    w = v * LIFT
    w = w * jnp.abs(w)
    w = w * jnp.abs(w)
    return w.astype(jnp.bfloat16)


def decode(u):
    u = u.astype(jnp.float32)
    r = lax.rsqrt(lax.rsqrt(jnp.maximum(jnp.abs(u), TINY))) * (1.0 / LIFT)
    return jnp.where(u < 0.0, -r, r)


def kernel(
    x_ref, t_ref, scale_ref, bias_ref, vis_ref, txt_ref,
    xb, tb, cb, db, vp, gp, sl, sr, rl, rr, core_out, core_in, y_out, y_in, x_out, x_in, ss, rs, own,
):
    blk = lax.axis_index("blk")
    grp = lax.axis_index("grp")
    z, y, core = grp // 4, (grp // 2) % 2, grp % 2
    right = (blk, ((z + 1) % 8) * 4 + y * 2 + core)
    left = (blk, ((z + 7) % 8) * 4 + y * 2 + core)
    across = (blk, z * 4 + (1 - y) * 2 + core)
    sibling = (blk, z * 4 + y * 2 + (1 - core))
    flip_down = 1 - (blk % 4 + 3) // 4
    up_blk = (blk + 1) % 8
    flip_up = 1 - (up_blk % 4 + 3) // 4
    down = ((blk + 7) % 8, z * 4 + ((y + flip_down) % 2) * 2 + core)
    up = (up_blk, z * 4 + ((y + flip_up) % 2) * 2 + core)

    own_image = pltpu.make_async_copy(x_ref, xb.at[pl.ds(0, ROWS)], own.at[0])
    own_text = pltpu.make_async_copy(t_ref, tb.at[pl.ds(0, ROWS)], own.at[1])
    own_image.start()
    own_text.start()

    barrier = pltpu.get_barrier_semaphore()
    for other in (right, left, across, sibling, down):
        pl.semaphore_signal(barrier, inc=1, device_id=other, device_id_type=MESH)
    pl.semaphore_wait(barrier, 5)

    copies = []

    def send(k, src, dst, device):
        copy = pltpu.make_async_remote_copy(
            src_ref=src, dst_ref=dst, send_sem=ss.at[k], recv_sem=rs.at[k],
            device_id=device, device_id_type=MESH,
        )
        copy.start()
        copies.append(copy)
        return copy

    low, high = pl.ds(0, HALF), pl.ds(HALF, HALF)

    def text(h, yy, cc):
        return pl.ds(512 * h + 256 * yy + 128 * cc, 128)

    zr, zl, tc = {}, {}, {}
    step = HALF // PIECES

    def go_round(i, p):
        at = pl.ds(ROWS * i + step * p, step)
        there = pl.ds(ROWS * i + HALF + step * p, step)
        if i <= 2:
            right_start, left_start = (0, HALF) if i == 1 else (HALF, 0)
            to_right, to_left = x_ref.at[pl.ds(right_start + step * p, step)], x_ref.at[pl.ds(left_start + step * p, step)]
        else:
            to_right = xb.at[pl.ds(ROWS * (i - 2) + step * p, step)]
            to_left = xb.at[pl.ds(ROWS * (i - 2) + HALF + step * p, step)]
        zr[i, p] = send(Z_RIGHT + PIECES * i + p, to_right, xb.at[at], right)
        zl[i, p] = send(Z_LEFT + PIECES * i + p, to_left, xb.at[there], left)

    for p in range(PIECES):
        go_round(1, p)
    ty0 = send(T_Y, t_ref, tb.at[text(0, 1, 0)], across)
    tx = send(T_X, t_ref, tb.at[text(1, 0, 0)], up)
    tc[0, 0] = send(T_CORE, t_ref, tb.at[text(0, 0, 1)], sibling)
    for p in range(PIECES):
        zr[1, p].wait_send()
        zl[1, p].wait_send()
        go_round(2, p)

    scale = scale_ref[0]
    slope = scale * (-LOG2E)
    shift = bias_ref[0] * LOG2E

    def arrive(i):
        for p in range(PIECES):
            zr[i, p].wait_recv()
            zl[i, p].wait_recv()
            if i + 2 <= 7:
                go_round(i + 2, p)

    def coefficients(start, rows, first, last):
        some = pl.ds(256 * first, 256 * (last - first))
        db[some, 0:rows] = lax.dot_general(
            tb[some, :], xb[start : start + rows, :], NT, preferred_element_type=jnp.float32
        )

        def tile(n, carry):
            texts = pl.ds(pl.multiple_of(n * 256, 256), 256)
            away = 1.0 + jnp.exp2(jnp.minimum(db[texts, 0:rows] * slope - shift, 126.0))
            c = pl.reciprocal(away, approx=True)
            c = c * (2.0 - away * c)
            if start == 0 and first == 0:
                row = lax.broadcasted_iota(jnp.int32, c.shape, 0) + n * 256
                col = lax.broadcasted_iota(jnp.int32, c.shape, 1)
                c = jnp.where((row == col) & (row < ROWS), c - 1.0, c)
            cb[texts, start : start + rows] = c.astype(jnp.bfloat16)
            return carry

        lax.fori_loop(first, last, tile, 0)

    def image_terms(start, rows):
        vp[start : start + rows, :] = lax.dot_general(
            cb[:, start : start + rows], tb[...], TN, preferred_element_type=jnp.float32
        )

    def text_terms(quarter):
        texts = pl.ds(256 * quarter, 256)
        gp[texts, :] = jnp.dot(cb[texts, :], xb[...], preferred_element_type=jnp.float32)

    vl, vr = {}, {}

    def pass_on(i):
        for p in range(PIECES):
            part = pl.ds(p * HALF // PIECES, HALF // PIECES)
            for way, (sent, out, came, to, k) in enumerate(
                ((vl, sl, rl, left, S_LEFT), (vr, sr, rr, right, S_RIGHT))
            ):
                total = vp[pl.ds(ROWS * i + HALF * way + p * HALF // PIECES, HALF // PIECES), :]
                if i <= 5:
                    sent[i + 2, p].wait_recv()
                    total = total + decode(came[i + 2, part, :])
                out[i, part, :] = code(total)
                sent[i, p] = send(k + PIECES * i + p, out.at[i, part], came.at[i, part], to)

    def code_rows(dst, src, src_start, count):
        def some(k, carry):
            at = pl.multiple_of(k * 64, 64)
            dst[pl.ds(at, 64), :] = code(src[pl.ds(src_start + at, 64), :])
            return carry

        lax.fori_loop(0, count // 64, some, 0)

    gc = {}

    def text_to_sibling(h, yy):
        code_rows(core_out.at[h, yy], gp, 512 * h + 256 * yy + 128, 128)
        gc[h, yy] = send(G_CORE + 2 * h + yy, core_out.at[h, yy], core_in.at[h, yy], sibling)

    gy = {}

    def text_across(h):
        gc[h, 1].wait_recv()
        for k in range(2):
            at = pl.ds(64 * k, 64)
            y_out[h, at, :] = code(gp[pl.ds(512 * h + 256 + 64 * k, 64), :] + decode(core_in[h, 1, at, :]))
            gy[h, k] = send(G_Y + 2 * h + k, y_out.at[h, at], y_in.at[h, at], across)

    def text_sum(h, k):
        at = pl.ds(64 * k, 64)
        if k == 0:
            gc[h, 0].wait_recv()
        gy[h, k].wait_recv()
        near = gp[pl.ds(512 * h + 64 * k, 64), :]
        return near + decode(core_in[h, 0, at, :]) + decode(y_in[h, at, :])

    own_text.wait()
    own_image.wait()
    arrive(1)
    tc[0, 0].wait_recv()
    coefficients(0, 256, 0, 1)
    arrive(2)
    ty0.wait_recv()
    far_low, far_high = pl.ds(768, HALF), pl.ds(768 + HALF, HALF)
    tx1 = send(T_X + 1, tb.at[pl.ds(256 + HALF, HALF)], tb.at[far_high], up)
    tc[0, 1] = send(T_CORE + 1, tb.at[text(0, 1, 0)], tb.at[text(0, 1, 1)], sibling)
    tc[0, 1].wait_recv()
    coefficients(0, 256, 1, 2)
    arrive(3)
    tx.wait_recv()
    ty1 = send(T_Y + 1, tb.at[pl.ds(512, HALF)], tb.at[far_low], across)
    tc[1, 0] = send(T_CORE + 2, tb.at[text(1, 0, 0)], tb.at[text(1, 0, 1)], sibling)
    coefficients(256, 256, 0, 2)
    tc[1, 0].wait_recv()
    coefficients(0, 256, 2, 3)
    coefficients(256, 256, 2, 3)
    arrive(4)
    ty1.wait_recv()
    tc[1, 1] = send(T_CORE + 3, tb.at[far_low], tb.at[pl.ds(896, HALF)], sibling)
    tx1.wait_recv()
    tc[1, 2] = send(T_CORE + 4, tb.at[far_high], tb.at[pl.ds(896 + HALF, HALF)], sibling)
    tc[1, 1].wait_recv()
    tc[1, 2].wait_recv()
    coefficients(0, 256, 3, 4)
    coefficients(256, 256, 3, 4)
    arrive(5)
    coefficients(512, 256, 0, 4)
    image_terms(512, 256)
    arrive(6)
    coefficients(768, 128, 0, 4)
    image_terms(768, 128)
    pass_on(6)
    arrive(7)
    coefficients(896, 128, 0, 4)
    image_terms(896, 128)
    pass_on(7)
    text_terms(3)
    text_to_sibling(1, 1)
    pass_on(4)
    text_across(1)
    text_terms(2)
    text_to_sibling(1, 0)
    pass_on(5)
    text_terms(1)
    text_to_sibling(0, 1)
    image_terms(256, 256)
    pass_on(2)
    gx = {}

    def text_down(k):
        at = pl.ds(64 * k, 64)
        x_out[at, :] = code(text_sum(1, k))
        gx[k] = send(G_X + k, x_out.at[at], x_in.at[at], down)

    text_down(0)
    text_across(0)
    text_terms(0)
    text_to_sibling(0, 0)
    pass_on(3)
    text_down(1)
    image_terms(0, 256)
    pass_on(1)
    for p in range(PIECES):
        vl[2, p].wait_recv()
        vr[2, p].wait_recv()
    vp[low, :] = vp[low, :] + decode(rr[2])
    vp[high, :] = vp[high, :] + decode(rl[2])
    for k in range(2):
        gp[pl.ds(64 * k, 64), :] = text_sum(0, k)
    for k in range(2):
        at = pl.ds(64 * k, 64)
        gx[k].wait_recv()
        txt_ref[at, :] = (gp[at, :] + decode(x_in[at, :]))
    for p in range(PIECES):
        vl[1, p].wait_recv()
        vr[1, p].wait_recv()
    vis_ref[low, :] = (vp[low, :] + decode(rl[1]))
    vis_ref[high, :] = (vp[high, :] + decode(rr[1]))
    for copy in copies:
        if not any(copy is zr[1, p] or copy is zl[1, p] for p in range(PIECES)):
            copy.wait_send()


def per_device(images, texts, scale, bias):
    rows, width = images.shape
    bf16, f32 = jnp.bfloat16, jnp.float32
    out = jax.ShapeDtypeStruct((rows, width), f32)
    vmem = pl.BlockSpec(memory_space=pltpu.VMEM)
    hbm = pl.BlockSpec(memory_space=pltpu.HBM)
    smem = pl.BlockSpec(memory_space=pltpu.SMEM)
    visual, textual = pl.pallas_call(
        kernel,
        out_shape=(out, out),
        in_specs=[hbm, hbm, smem, smem],
        out_specs=(vmem, vmem),
        scratch_shapes=[
            pltpu.VMEM((1024, width), bf16),
            pltpu.VMEM((1024, width), bf16),
            pltpu.VMEM((1024, 1024), bf16),
            pltpu.VMEM((1024, 256), f32),
            pltpu.VMEM((1024, width), f32),
            pltpu.VMEM((1024, width), f32),
            pltpu.VMEM((8, HALF, width), bf16),
            pltpu.VMEM((8, HALF, width), bf16),
            pltpu.VMEM((8, HALF, width), bf16),
            pltpu.VMEM((8, HALF, width), bf16),
            pltpu.VMEM((2, 2, ROWS, width), bf16),
            pltpu.VMEM((2, 2, ROWS, width), bf16),
            pltpu.VMEM((2, ROWS, width), bf16),
            pltpu.VMEM((2, ROWS, width), bf16),
            pltpu.VMEM((ROWS, width), bf16),
            pltpu.VMEM((ROWS, width), bf16),
            pltpu.SemaphoreType.DMA((N_SEM,)),
            pltpu.SemaphoreType.DMA((N_SEM,)),
            pltpu.SemaphoreType.DMA((2,)),
        ],
        compiler_params=pltpu.CompilerParams(
            collective_id=0, has_side_effects=True, vmem_limit_bytes=48 * 1024 * 1024
        ),
        cost_estimate=pl.CostEstimate(
            flops=6 * 1024 * 1024 * width, bytes_accessed=12 * rows * width, transcendentals=2 * 1024 * 1024
        ),
    )(pltpu.with_memory_space_constraint(images, pltpu.HBM), pltpu.with_memory_space_constraint(texts, pltpu.HBM), scale, bias)
    return scale[0] * visual, scale[0] * textual


def solution(mesh):
    spec = P(("blk", "grp"), None)
    return jax.shard_map(
        per_device,
        mesh=mesh,
        in_specs=(spec, spec, P(), P()),
        out_specs=(spec, spec),
        check_vma=False,
    )
```

```python
import functools

import jax
import jax.numpy as jnp
from jax import lax
from jax.experimental import pallas as pl
from jax.experimental.pallas import tpu as pltpu
from jax.sharding import PartitionSpec as P

MESH = pl.DeviceIdType.MESH
LIFT = 2.0**18
TINY = 1e-37
LOG2E = 1.4426950408889634
HALF = 64
ROWS = 128
NT = (((1,), (1,)), ((), ()))
TN = (((0,), (0,)), ((), ()))

Z_RIGHT, Z_LEFT = 0, 16
S_RIGHT, S_LEFT = 32, 48
T_CORE, T_Y, T_X = 64, 69, 71
G_CORE, G_Y, G_X = 73, 77, 81
N_SEM = 83
PIECES = 2


def code(v):
    w = v * LIFT
    w = w * jnp.abs(w)
    w = w * jnp.abs(w)
    return w.astype(jnp.bfloat16)


def decode(u):
    u = u.astype(jnp.float32)
    r = lax.rsqrt(lax.rsqrt(jnp.maximum(jnp.abs(u), TINY))) * (1.0 / LIFT)
    return jnp.where(u < 0.0, -r, r)


def kernel(
    x_ref, t_ref, scale_ref, bias_ref, vis_ref, txt_ref,
    xb, tb, cb, db, vp, gp, sl, sr, rl, rr, core_out, core_in, y_out, y_in, x_out, x_in, ss, rs, own,
):
    blk = lax.axis_index("blk")
    grp = lax.axis_index("grp")
    z, y, core = grp // 4, (grp // 2) % 2, grp % 2
    right = (blk, ((z + 1) % 8) * 4 + y * 2 + core)
    left = (blk, ((z + 7) % 8) * 4 + y * 2 + core)
    across = (blk, z * 4 + (1 - y) * 2 + core)
    sibling = (blk, z * 4 + y * 2 + (1 - core))
    flip_down = 1 - (blk % 4 + 3) // 4
    up_blk = (blk + 1) % 8
    flip_up = 1 - (up_blk % 4 + 3) // 4
    down = ((blk + 7) % 8, z * 4 + ((y + flip_down) % 2) * 2 + core)
    up = (up_blk, z * 4 + ((y + flip_up) % 2) * 2 + core)

    own_image = pltpu.make_async_copy(x_ref, xb.at[pl.ds(0, ROWS)], own.at[0])
    own_text = pltpu.make_async_copy(t_ref, tb.at[pl.ds(0, ROWS)], own.at[1])
    own_image.start()
    own_text.start()

    barrier = pltpu.get_barrier_semaphore()
    for other in (right, left, across, sibling, down):
        pl.semaphore_signal(barrier, inc=1, device_id=other, device_id_type=MESH)
    pl.semaphore_wait(barrier, 5)

    copies = []

    def send(k, src, dst, device):
        copy = pltpu.make_async_remote_copy(
            src_ref=src, dst_ref=dst, send_sem=ss.at[k], recv_sem=rs.at[k],
            device_id=device, device_id_type=MESH,
        )
        copy.start()
        copies.append(copy)
        return copy

    low, high = pl.ds(0, HALF), pl.ds(HALF, HALF)

    def text(h, yy, cc):
        return pl.ds(512 * h + 256 * yy + 128 * cc, 128)

    zr, zl, tc = {}, {}, {}
    step = HALF // PIECES

    def go_round(i, p):
        at = pl.ds(ROWS * i + step * p, step)
        there = pl.ds(ROWS * i + HALF + step * p, step)
        if i <= 2:
            right_start, left_start = (0, HALF) if i == 1 else (HALF, 0)
            to_right, to_left = x_ref.at[pl.ds(right_start + step * p, step)], x_ref.at[pl.ds(left_start + step * p, step)]
        else:
            to_right = xb.at[pl.ds(ROWS * (i - 2) + step * p, step)]
            to_left = xb.at[pl.ds(ROWS * (i - 2) + HALF + step * p, step)]
        zr[i, p] = send(Z_RIGHT + PIECES * i + p, to_right, xb.at[at], right)
        zl[i, p] = send(Z_LEFT + PIECES * i + p, to_left, xb.at[there], left)

    for p in range(PIECES):
        go_round(1, p)
    ty0 = send(T_Y, t_ref, tb.at[text(0, 1, 0)], across)
    tx = send(T_X, t_ref, tb.at[text(1, 0, 0)], up)
    tc[0, 0] = send(T_CORE, t_ref, tb.at[text(0, 0, 1)], sibling)
    for p in range(PIECES):
        zr[1, p].wait_send()
        zl[1, p].wait_send()
        go_round(2, p)

    scale = scale_ref[0]
    slope = scale * (-LOG2E)
    shift = bias_ref[0] * LOG2E

    def arrive(i):
        for p in range(PIECES):
            zr[i, p].wait_recv()
            zl[i, p].wait_recv()
            if i + 2 <= 7:
                go_round(i + 2, p)

    def coefficients(start, rows, first, last):
        some = pl.ds(256 * first, 256 * (last - first))
        db[some, 0:rows] = lax.dot_general(
            tb[some, :], xb[start : start + rows, :], NT, preferred_element_type=jnp.float32
        )

        def tile(n, carry):
            texts = pl.ds(pl.multiple_of(n * 256, 256), 256)
            away = 1.0 + jnp.exp2(jnp.minimum(db[texts, 0:rows] * slope - shift, 126.0))
            c = pl.reciprocal(away, approx=True)
            c = c * (2.0 - away * c)
            if start == 0 and first == 0:
                row = lax.broadcasted_iota(jnp.int32, c.shape, 0) + n * 256
                col = lax.broadcasted_iota(jnp.int32, c.shape, 1)
                c = jnp.where((row == col) & (row < ROWS), c - 1.0, c)
            cb[texts, start : start + rows] = c.astype(jnp.bfloat16)
            return carry

        lax.fori_loop(first, last, tile, 0)

    def image_terms(start, rows):
        vp[start : start + rows, :] = lax.dot_general(
            cb[:, start : start + rows], tb[...], TN, preferred_element_type=jnp.float32
        )

    def text_terms(quarter):
        texts = pl.ds(256 * quarter, 256)
        gp[texts, :] = jnp.dot(cb[texts, :], xb[...], preferred_element_type=jnp.float32)

    vl, vr = {}, {}

    def pass_on(i):
        for p in range(PIECES):
            part = pl.ds(p * HALF // PIECES, HALF // PIECES)
            for way, (sent, out, came, to, k) in enumerate(
                ((vl, sl, rl, left, S_LEFT), (vr, sr, rr, right, S_RIGHT))
            ):
                total = vp[pl.ds(ROWS * i + HALF * way + p * HALF // PIECES, HALF // PIECES), :]
                if i <= 5:
                    sent[i + 2, p].wait_recv()
                    total = total + decode(came[i + 2, part, :])
                out[i, part, :] = code(total)
                sent[i, p] = send(k + PIECES * i + p, out.at[i, part], came.at[i, part], to)

    def code_rows(dst, src, src_start, count):
        def some(k, carry):
            at = pl.multiple_of(k * 64, 64)
            dst[pl.ds(at, 64), :] = code(src[pl.ds(src_start + at, 64), :])
            return carry

        lax.fori_loop(0, count // 64, some, 0)

    gc = {}

    def text_to_sibling(h, yy):
        code_rows(core_out.at[h, yy], gp, 512 * h + 256 * yy + 128, 128)
        gc[h, yy] = send(G_CORE + 2 * h + yy, core_out.at[h, yy], core_in.at[h, yy], sibling)

    gy = {}

    def text_across(h):
        gc[h, 1].wait_recv()
        for k in range(2):
            at = pl.ds(64 * k, 64)
            y_out[h, at, :] = code(gp[pl.ds(512 * h + 256 + 64 * k, 64), :] + decode(core_in[h, 1, at, :]))
            gy[h, k] = send(G_Y + 2 * h + k, y_out.at[h, at], y_in.at[h, at], across)

    def text_sum(h, k):
        at = pl.ds(64 * k, 64)
        if k == 0:
            gc[h, 0].wait_recv()
        gy[h, k].wait_recv()
        near = gp[pl.ds(512 * h + 64 * k, 64), :]
        return near + decode(core_in[h, 0, at, :]) + decode(y_in[h, at, :])

    own_text.wait()
    own_image.wait()
    arrive(1)
    tc[0, 0].wait_recv()
    coefficients(0, 256, 0, 1)
    arrive(2)
    ty0.wait_recv()
    far_low, far_high = pl.ds(768, HALF), pl.ds(768 + HALF, HALF)
    tx1 = send(T_X + 1, tb.at[pl.ds(256 + HALF, HALF)], tb.at[far_high], up)
    tc[0, 1] = send(T_CORE + 1, tb.at[text(0, 1, 0)], tb.at[text(0, 1, 1)], sibling)
    tx.wait_recv()
    ty1 = send(T_Y + 1, tb.at[pl.ds(512, HALF)], tb.at[far_low], across)
    tc[1, 0] = send(T_CORE + 2, tb.at[text(1, 0, 0)], tb.at[text(1, 0, 1)], sibling)
    tc[0, 1].wait_recv()
    tc[1, 0].wait_recv()
    coefficients(0, 256, 1, 3)
    arrive(3)
    coefficients(256, 256, 0, 3)
    arrive(4)
    ty1.wait_recv()
    tc[1, 1] = send(T_CORE + 3, tb.at[far_low], tb.at[pl.ds(896, HALF)], sibling)
    tx1.wait_recv()
    tc[1, 2] = send(T_CORE + 4, tb.at[far_high], tb.at[pl.ds(896 + HALF, HALF)], sibling)
    tc[1, 1].wait_recv()
    tc[1, 2].wait_recv()
    coefficients(0, 256, 3, 4)
    coefficients(256, 256, 3, 4)
    arrive(5)
    coefficients(512, 256, 0, 4)
    image_terms(512, 256)
    arrive(6)
    coefficients(768, 128, 0, 4)
    image_terms(768, 128)
    pass_on(6)
    arrive(7)
    coefficients(896, 128, 0, 4)
    image_terms(896, 128)
    pass_on(7)
    text_terms(3)
    text_to_sibling(1, 1)
    pass_on(4)
    text_across(1)
    text_terms(2)
    text_to_sibling(1, 0)
    pass_on(5)
    text_terms(1)
    text_to_sibling(0, 1)
    image_terms(256, 256)
    pass_on(2)
    gx = {}

    def text_down(k):
        at = pl.ds(64 * k, 64)
        x_out[at, :] = code(text_sum(1, k))
        gx[k] = send(G_X + k, x_out.at[at], x_in.at[at], down)

    text_down(0)
    text_across(0)
    text_terms(0)
    text_to_sibling(0, 0)
    pass_on(3)
    text_down(1)
    image_terms(0, 256)
    pass_on(1)
    for p in range(PIECES):
        vl[2, p].wait_recv()
        vr[2, p].wait_recv()
    vp[low, :] = vp[low, :] + decode(rr[2])
    vp[high, :] = vp[high, :] + decode(rl[2])
    for k in range(2):
        gp[pl.ds(64 * k, 64), :] = text_sum(0, k)
    for k in range(2):
        at = pl.ds(64 * k, 64)
        gx[k].wait_recv()
        txt_ref[at, :] = (gp[at, :] + decode(x_in[at, :]))
    for p in range(PIECES):
        vl[1, p].wait_recv()
        vr[1, p].wait_recv()
    vis_ref[low, :] = (vp[low, :] + decode(rl[1]))
    vis_ref[high, :] = (vp[high, :] + decode(rr[1]))
    for copy in copies:
        if not any(copy is zr[1, p] or copy is zl[1, p] for p in range(PIECES)):
            copy.wait_send()


def per_device(images, texts, scale, bias):
    rows, width = images.shape
    bf16, f32 = jnp.bfloat16, jnp.float32
    out = jax.ShapeDtypeStruct((rows, width), f32)
    vmem = pl.BlockSpec(memory_space=pltpu.VMEM)
    hbm = pl.BlockSpec(memory_space=pltpu.HBM)
    smem = pl.BlockSpec(memory_space=pltpu.SMEM)
    visual, textual = pl.pallas_call(
        kernel,
        out_shape=(out, out),
        in_specs=[hbm, hbm, smem, smem],
        out_specs=(vmem, vmem),
        scratch_shapes=[
            pltpu.VMEM((1024, width), bf16),
            pltpu.VMEM((1024, width), bf16),
            pltpu.VMEM((1024, 1024), bf16),
            pltpu.VMEM((1024, 256), f32),
            pltpu.VMEM((1024, width), f32),
            pltpu.VMEM((1024, width), f32),
            pltpu.VMEM((8, HALF, width), bf16),
            pltpu.VMEM((8, HALF, width), bf16),
            pltpu.VMEM((8, HALF, width), bf16),
            pltpu.VMEM((8, HALF, width), bf16),
            pltpu.VMEM((2, 2, ROWS, width), bf16),
            pltpu.VMEM((2, 2, ROWS, width), bf16),
            pltpu.VMEM((2, ROWS, width), bf16),
            pltpu.VMEM((2, ROWS, width), bf16),
            pltpu.VMEM((ROWS, width), bf16),
            pltpu.VMEM((ROWS, width), bf16),
            pltpu.SemaphoreType.DMA((N_SEM,)),
            pltpu.SemaphoreType.DMA((N_SEM,)),
            pltpu.SemaphoreType.DMA((2,)),
        ],
        compiler_params=pltpu.CompilerParams(
            collective_id=0, has_side_effects=True, vmem_limit_bytes=48 * 1024 * 1024
        ),
        cost_estimate=pl.CostEstimate(
            flops=6 * 1024 * 1024 * width, bytes_accessed=12 * rows * width, transcendentals=2 * 1024 * 1024
        ),
    )(pltpu.with_memory_space_constraint(images, pltpu.HBM), pltpu.with_memory_space_constraint(texts, pltpu.HBM), scale, bias)
    return scale[0] * visual, scale[0] * textual


def solution(mesh):
    spec = P(("blk", "grp"), None)
    return jax.shard_map(
        per_device,
        mesh=mesh,
        in_specs=(spec, spec, P(), P()),
        out_specs=(spec, spec),
        check_vma=False,
    )
```

```python
import functools

import jax
import jax.numpy as jnp
from jax import lax
from jax.experimental import pallas as pl
from jax.experimental.pallas import tpu as pltpu
from jax.sharding import PartitionSpec as P

MESH = pl.DeviceIdType.MESH
LIFT = 2.0**18
TINY = 1e-37
LOG2E = 1.4426950408889634
HALF = 64
ROWS = 128
NT = (((1,), (1,)), ((), ()))
TN = (((0,), (0,)), ((), ()))

Z_RIGHT, Z_LEFT = 0, 16
S_RIGHT, S_LEFT = 32, 48
T_CORE, T_Y, T_X = 64, 69, 71
G_CORE, G_Y, G_X = 73, 77, 81
N_SEM = 83
PIECES = 2


def code(v):
    w = v * LIFT
    w = w * jnp.abs(w)
    w = w * jnp.abs(w)
    return w.astype(jnp.bfloat16)


def decode(u):
    u = u.astype(jnp.float32)
    r = lax.rsqrt(lax.rsqrt(jnp.maximum(jnp.abs(u), TINY))) * (1.0 / LIFT)
    return jnp.where(u < 0.0, -r, r)


def kernel(
    x_ref, t_ref, scale_ref, bias_ref, vis_ref, txt_ref,
    xb, tb, cb, db, vp, gp, sl, sr, rl, rr, core_out, core_in, y_out, y_in, x_out, x_in, ss, rs, own,
):
    blk = lax.axis_index("blk")
    grp = lax.axis_index("grp")
    z, y, core = grp // 4, (grp // 2) % 2, grp % 2
    right = (blk, ((z + 1) % 8) * 4 + y * 2 + core)
    left = (blk, ((z + 7) % 8) * 4 + y * 2 + core)
    across = (blk, z * 4 + (1 - y) * 2 + core)
    sibling = (blk, z * 4 + y * 2 + (1 - core))
    flip_down = 1 - (blk % 4 + 3) // 4
    up_blk = (blk + 1) % 8
    flip_up = 1 - (up_blk % 4 + 3) // 4
    down = ((blk + 7) % 8, z * 4 + ((y + flip_down) % 2) * 2 + core)
    up = (up_blk, z * 4 + ((y + flip_up) % 2) * 2 + core)

    own_image = pltpu.make_async_copy(x_ref, xb.at[pl.ds(0, ROWS)], own.at[0])
    own_text = pltpu.make_async_copy(t_ref, tb.at[pl.ds(0, ROWS)], own.at[1])
    own_image.start()
    own_text.start()

    barrier = pltpu.get_barrier_semaphore()
    for other in (right, left, across, sibling, down):
        pl.semaphore_signal(barrier, inc=1, device_id=other, device_id_type=MESH)
    pl.semaphore_wait(barrier, 5)

    copies = []

    def send(k, src, dst, device):
        copy = pltpu.make_async_remote_copy(
            src_ref=src, dst_ref=dst, send_sem=ss.at[k], recv_sem=rs.at[k],
            device_id=device, device_id_type=MESH,
        )
        copy.start()
        copies.append(copy)
        return copy

    low, high = pl.ds(0, HALF), pl.ds(HALF, HALF)

    def text(h, yy, cc):
        return pl.ds(512 * h + 256 * yy + 128 * cc, 128)

    zr, zl, tc = {}, {}, {}
    step = HALF // PIECES

    def go_round(i, p):
        at = pl.ds(ROWS * i + step * p, step)
        there = pl.ds(ROWS * i + HALF + step * p, step)
        if i <= 2:
            right_start, left_start = (0, HALF) if i == 1 else (HALF, 0)
            to_right, to_left = x_ref.at[pl.ds(right_start + step * p, step)], x_ref.at[pl.ds(left_start + step * p, step)]
        else:
            to_right = xb.at[pl.ds(ROWS * (i - 2) + step * p, step)]
            to_left = xb.at[pl.ds(ROWS * (i - 2) + HALF + step * p, step)]
        zr[i, p] = send(Z_RIGHT + PIECES * i + p, to_right, xb.at[at], right)
        zl[i, p] = send(Z_LEFT + PIECES * i + p, to_left, xb.at[there], left)

    for p in range(PIECES):
        go_round(1, p)
    ty0 = send(T_Y, t_ref, tb.at[text(0, 1, 0)], across)
    tx = send(T_X, t_ref, tb.at[text(1, 0, 0)], up)
    tc[0, 0] = send(T_CORE, t_ref, tb.at[text(0, 0, 1)], sibling)
    for p in range(PIECES):
        zr[1, p].wait_send()
        zl[1, p].wait_send()
        go_round(2, p)

    scale = scale_ref[0]
    slope = scale * (-LOG2E)
    shift = bias_ref[0] * LOG2E

    def arrive(i):
        for p in range(PIECES):
            zr[i, p].wait_recv()
            zl[i, p].wait_recv()
            if i + 2 <= 7:
                go_round(i + 2, p)

    def coefficients(start, rows, first, last):
        some = pl.ds(256 * first, 256 * (last - first))
        db[some, 0:rows] = lax.dot_general(
            tb[some, :], xb[start : start + rows, :], NT, preferred_element_type=jnp.float32
        )

        def tile(n, carry):
            texts = pl.ds(pl.multiple_of(n * 256, 256), 256)
            away = 1.0 + jnp.exp2(jnp.minimum(db[texts, 0:rows] * slope - shift, 126.0))
            c = pl.reciprocal(away, approx=True)
            c = c * (2.0 - away * c)
            if start == 0 and first == 0:
                row = lax.broadcasted_iota(jnp.int32, c.shape, 0) + n * 256
                col = lax.broadcasted_iota(jnp.int32, c.shape, 1)
                c = jnp.where((row == col) & (row < ROWS), c - 1.0, c)
            cb[texts, start : start + rows] = c.astype(jnp.bfloat16)
            return carry

        lax.fori_loop(first, last, tile, 0)

    def image_terms(start, rows, first, last):
        texts = pl.ds(256 * first, 256 * (last - first))
        term = lax.dot_general(
            cb[texts, start : start + rows], tb[texts, :], TN, preferred_element_type=jnp.float32
        )
        if first > 0:
            term = vp[start : start + rows, :] + term
        vp[start : start + rows, :] = term

    def text_terms(quarter):
        texts = pl.ds(256 * quarter, 256)
        gp[texts, :] = jnp.dot(cb[texts, :], xb[...], preferred_element_type=jnp.float32)

    vl, vr = {}, {}

    def pass_on(i):
        for p in range(PIECES):
            part = pl.ds(p * HALF // PIECES, HALF // PIECES)
            for way, (sent, out, came, to, k) in enumerate(
                ((vl, sl, rl, left, S_LEFT), (vr, sr, rr, right, S_RIGHT))
            ):
                total = vp[pl.ds(ROWS * i + HALF * way + p * HALF // PIECES, HALF // PIECES), :]
                if i <= 5:
                    sent[i + 2, p].wait_recv()
                    total = total + decode(came[i + 2, part, :])
                out[i, part, :] = code(total)
                sent[i, p] = send(k + PIECES * i + p, out.at[i, part], came.at[i, part], to)

    def code_rows(dst, src, src_start, count):
        def some(k, carry):
            at = pl.multiple_of(k * 64, 64)
            dst[pl.ds(at, 64), :] = code(src[pl.ds(src_start + at, 64), :])
            return carry

        lax.fori_loop(0, count // 64, some, 0)

    gc = {}

    def text_to_sibling(h, yy):
        code_rows(core_out.at[h, yy], gp, 512 * h + 256 * yy + 128, 128)
        gc[h, yy] = send(G_CORE + 2 * h + yy, core_out.at[h, yy], core_in.at[h, yy], sibling)

    gy = {}

    def text_across(h):
        gc[h, 1].wait_recv()
        for k in range(2):
            at = pl.ds(64 * k, 64)
            y_out[h, at, :] = code(gp[pl.ds(512 * h + 256 + 64 * k, 64), :] + decode(core_in[h, 1, at, :]))
            gy[h, k] = send(G_Y + 2 * h + k, y_out.at[h, at], y_in.at[h, at], across)

    def text_sum(h, k):
        at = pl.ds(64 * k, 64)
        if k == 0:
            gc[h, 0].wait_recv()
        gy[h, k].wait_recv()
        near = gp[pl.ds(512 * h + 64 * k, 64), :]
        return near + decode(core_in[h, 0, at, :]) + decode(y_in[h, at, :])

    own_text.wait()
    own_image.wait()
    arrive(1)
    tc[0, 0].wait_recv()
    coefficients(0, 256, 0, 1)
    arrive(2)
    ty0.wait_recv()
    far_low, far_high = pl.ds(768, HALF), pl.ds(768 + HALF, HALF)
    tx1 = send(T_X + 1, tb.at[pl.ds(256 + HALF, HALF)], tb.at[far_high], up)
    tc[0, 1] = send(T_CORE + 1, tb.at[text(0, 1, 0)], tb.at[text(0, 1, 1)], sibling)
    tx.wait_recv()
    ty1 = send(T_Y + 1, tb.at[pl.ds(512, HALF)], tb.at[far_low], across)
    tc[1, 0] = send(T_CORE + 2, tb.at[text(1, 0, 0)], tb.at[text(1, 0, 1)], sibling)
    tc[0, 1].wait_recv()
    tc[1, 0].wait_recv()
    coefficients(0, 256, 1, 3)
    arrive(3)
    coefficients(256, 256, 0, 3)
    image_terms(0, 512, 0, 2)
    arrive(4)
    ty1.wait_recv()
    tc[1, 1] = send(T_CORE + 3, tb.at[far_low], tb.at[pl.ds(896, HALF)], sibling)
    tx1.wait_recv()
    tc[1, 2] = send(T_CORE + 4, tb.at[far_high], tb.at[pl.ds(896 + HALF, HALF)], sibling)
    tc[1, 1].wait_recv()
    tc[1, 2].wait_recv()
    coefficients(0, 256, 3, 4)
    coefficients(256, 256, 3, 4)
    image_terms(256, 256, 2, 4)
    arrive(5)
    coefficients(512, 256, 0, 4)
    image_terms(512, 256, 0, 4)
    arrive(6)
    coefficients(768, 128, 0, 4)
    image_terms(768, 128, 0, 4)
    pass_on(6)
    arrive(7)
    coefficients(896, 128, 0, 4)
    image_terms(896, 128, 0, 4)
    pass_on(7)
    text_terms(3)
    text_to_sibling(1, 1)
    pass_on(4)
    text_across(1)
    text_terms(2)
    text_to_sibling(1, 0)
    pass_on(5)
    text_terms(1)
    text_to_sibling(0, 1)
    pass_on(2)
    gx = {}

    def text_down(k):
        at = pl.ds(64 * k, 64)
        x_out[at, :] = code(text_sum(1, k))
        gx[k] = send(G_X + k, x_out.at[at], x_in.at[at], down)

    text_down(0)
    text_across(0)
    text_terms(0)
    text_to_sibling(0, 0)
    pass_on(3)
    text_down(1)
    image_terms(0, 256, 2, 4)
    pass_on(1)
    for p in range(PIECES):
        vl[2, p].wait_recv()
        vr[2, p].wait_recv()
    vp[low, :] = vp[low, :] + decode(rr[2])
    vp[high, :] = vp[high, :] + decode(rl[2])
    for k in range(2):
        gp[pl.ds(64 * k, 64), :] = text_sum(0, k)
    for k in range(2):
        at = pl.ds(64 * k, 64)
        gx[k].wait_recv()
        txt_ref[at, :] = (gp[at, :] + decode(x_in[at, :]))
    for p in range(PIECES):
        vl[1, p].wait_recv()
        vr[1, p].wait_recv()
    vis_ref[low, :] = (vp[low, :] + decode(rl[1]))
    vis_ref[high, :] = (vp[high, :] + decode(rr[1]))
    for copy in copies:
        if not any(copy is zr[1, p] or copy is zl[1, p] for p in range(PIECES)):
            copy.wait_send()


def per_device(images, texts, scale, bias):
    rows, width = images.shape
    bf16, f32 = jnp.bfloat16, jnp.float32
    out = jax.ShapeDtypeStruct((rows, width), f32)
    vmem = pl.BlockSpec(memory_space=pltpu.VMEM)
    hbm = pl.BlockSpec(memory_space=pltpu.HBM)
    smem = pl.BlockSpec(memory_space=pltpu.SMEM)
    visual, textual = pl.pallas_call(
        kernel,
        out_shape=(out, out),
        in_specs=[hbm, hbm, smem, smem],
        out_specs=(vmem, vmem),
        scratch_shapes=[
            pltpu.VMEM((1024, width), bf16),
            pltpu.VMEM((1024, width), bf16),
            pltpu.VMEM((1024, 1024), bf16),
            pltpu.VMEM((1024, 256), f32),
            pltpu.VMEM((1024, width), f32),
            pltpu.VMEM((1024, width), f32),
            pltpu.VMEM((8, HALF, width), bf16),
            pltpu.VMEM((8, HALF, width), bf16),
            pltpu.VMEM((8, HALF, width), bf16),
            pltpu.VMEM((8, HALF, width), bf16),
            pltpu.VMEM((2, 2, ROWS, width), bf16),
            pltpu.VMEM((2, 2, ROWS, width), bf16),
            pltpu.VMEM((2, ROWS, width), bf16),
            pltpu.VMEM((2, ROWS, width), bf16),
            pltpu.VMEM((ROWS, width), bf16),
            pltpu.VMEM((ROWS, width), bf16),
            pltpu.SemaphoreType.DMA((N_SEM,)),
            pltpu.SemaphoreType.DMA((N_SEM,)),
            pltpu.SemaphoreType.DMA((2,)),
        ],
        compiler_params=pltpu.CompilerParams(
            collective_id=0, has_side_effects=True, vmem_limit_bytes=48 * 1024 * 1024
        ),
        cost_estimate=pl.CostEstimate(
            flops=6 * 1024 * 1024 * width, bytes_accessed=12 * rows * width, transcendentals=2 * 1024 * 1024
        ),
    )(pltpu.with_memory_space_constraint(images, pltpu.HBM), pltpu.with_memory_space_constraint(texts, pltpu.HBM), scale, bias)
    return scale[0] * visual, scale[0] * textual


def solution(mesh):
    spec = P(("blk", "grp"), None)
    return jax.shard_map(
        per_device,
        mesh=mesh,
        in_specs=(spec, spec, P(), P()),
        out_specs=(spec, spec),
        check_vma=False,
    )
```

```python
import functools

import jax
import jax.numpy as jnp
from jax import lax
from jax.experimental import pallas as pl
from jax.experimental.pallas import tpu as pltpu
from jax.sharding import PartitionSpec as P

MESH = pl.DeviceIdType.MESH
LIFT = 2.0**18
TINY = 1e-37
LOG2E = 1.4426950408889634
HALF = 64
ROWS = 128
NT = (((1,), (1,)), ((), ()))
TN = (((0,), (0,)), ((), ()))

Z_RIGHT, Z_LEFT = 0, 16
S_RIGHT, S_LEFT = 32, 48
T_CORE, T_Y, T_X = 64, 69, 71
G_CORE, G_Y, G_X = 73, 77, 81
N_SEM = 83
PIECES = 2


def code(v):
    w = v * LIFT
    w = w * jnp.abs(w)
    w = w * jnp.abs(w)
    return w.astype(jnp.bfloat16)


def decode(u):
    u = u.astype(jnp.float32)
    r = lax.rsqrt(lax.rsqrt(jnp.maximum(jnp.abs(u), TINY))) * (1.0 / LIFT)
    return jnp.where(u < 0.0, -r, r)


def kernel(
    x_ref, t_ref, scale_ref, bias_ref, vis_ref, txt_ref,
    xb, tb, cb, db, vp, gp, sl, sr, rl, rr, core_out, core_in, y_out, y_in, x_out, x_in, ss, rs, own,
):
    blk = lax.axis_index("blk")
    grp = lax.axis_index("grp")
    z, y, core = grp // 4, (grp // 2) % 2, grp % 2
    right = (blk, ((z + 1) % 8) * 4 + y * 2 + core)
    left = (blk, ((z + 7) % 8) * 4 + y * 2 + core)
    across = (blk, z * 4 + (1 - y) * 2 + core)
    sibling = (blk, z * 4 + y * 2 + (1 - core))
    flip_down = 1 - (blk % 4 + 3) // 4
    up_blk = (blk + 1) % 8
    flip_up = 1 - (up_blk % 4 + 3) // 4
    down = ((blk + 7) % 8, z * 4 + ((y + flip_down) % 2) * 2 + core)
    up = (up_blk, z * 4 + ((y + flip_up) % 2) * 2 + core)

    barrier = pltpu.get_barrier_semaphore()
    for other in (right, left, across, sibling, down):
        pl.semaphore_signal(barrier, inc=1, device_id=other, device_id_type=MESH)
    own_image = pltpu.make_async_copy(x_ref, xb.at[pl.ds(0, ROWS)], own.at[0])
    own_text = pltpu.make_async_copy(t_ref, tb.at[pl.ds(0, ROWS)], own.at[1])
    own_image.start()
    own_text.start()
    pl.semaphore_wait(barrier, 5)

    copies = []

    def send(k, src, dst, device):
        copy = pltpu.make_async_remote_copy(
            src_ref=src, dst_ref=dst, send_sem=ss.at[k], recv_sem=rs.at[k],
            device_id=device, device_id_type=MESH,
        )
        copy.start()
        copies.append(copy)
        return copy

    low, high = pl.ds(0, HALF), pl.ds(HALF, HALF)

    def text(h, yy, cc):
        return pl.ds(512 * h + 256 * yy + 128 * cc, 128)

    zr, zl, tc = {}, {}, {}
    step = HALF // PIECES

    def go_round(i, p):
        at = pl.ds(ROWS * i + step * p, step)
        there = pl.ds(ROWS * i + HALF + step * p, step)
        if i <= 2:
            right_start, left_start = (0, HALF) if i == 1 else (HALF, 0)
            to_right, to_left = x_ref.at[pl.ds(right_start + step * p, step)], x_ref.at[pl.ds(left_start + step * p, step)]
        else:
            to_right = xb.at[pl.ds(ROWS * (i - 2) + step * p, step)]
            to_left = xb.at[pl.ds(ROWS * (i - 2) + HALF + step * p, step)]
        zr[i, p] = send(Z_RIGHT + PIECES * i + p, to_right, xb.at[at], right)
        zl[i, p] = send(Z_LEFT + PIECES * i + p, to_left, xb.at[there], left)

    for p in range(PIECES):
        go_round(1, p)
    ty0 = send(T_Y, t_ref, tb.at[text(0, 1, 0)], across)
    tx = send(T_X, t_ref, tb.at[text(1, 0, 0)], up)
    tc[0, 0] = send(T_CORE, t_ref, tb.at[text(0, 0, 1)], sibling)
    for p in range(PIECES):
        zr[1, p].wait_send()
        zl[1, p].wait_send()
        go_round(2, p)

    scale = scale_ref[0]
    slope = scale * (-LOG2E)
    shift = bias_ref[0] * LOG2E

    def arrive(i):
        for p in range(PIECES):
            zr[i, p].wait_recv()
            zl[i, p].wait_recv()
            if i + 2 <= 7:
                go_round(i + 2, p)

    def coefficients(start, rows, first, last):
        some = pl.ds(256 * first, 256 * (last - first))
        db[some, 0:rows] = lax.dot_general(
            tb[some, :], xb[start : start + rows, :], NT, preferred_element_type=jnp.float32
        )

        def tile(n, carry):
            texts = pl.ds(pl.multiple_of(n * 256, 256), 256)
            away = 1.0 + jnp.exp2(jnp.minimum(db[texts, 0:rows] * slope - shift, 126.0))
            c = pl.reciprocal(away, approx=True)
            c = c * (2.0 - away * c)
            if start == 0 and first == 0:
                row = lax.broadcasted_iota(jnp.int32, c.shape, 0) + n * 256
                col = lax.broadcasted_iota(jnp.int32, c.shape, 1)
                c = jnp.where((row == col) & (row < ROWS), c - 1.0, c)
            cb[texts, start : start + rows] = c.astype(jnp.bfloat16)
            return carry

        lax.fori_loop(first, last, tile, 0)

    def image_terms(start, rows, first, last):
        texts = pl.ds(256 * first, 256 * (last - first))
        term = lax.dot_general(
            cb[texts, start : start + rows], tb[texts, :], TN, preferred_element_type=jnp.float32
        )
        if first > 0:
            term = vp[start : start + rows, :] + term
        vp[start : start + rows, :] = term

    def text_terms(quarter, part):
        texts = pl.ds(256 * quarter, 256)
        cols = (pl.ds(0, 640), pl.ds(640, 512))[part]
        gp[texts, cols] = jnp.dot(cb[texts, :], xb[:, cols], preferred_element_type=jnp.float32)

    vl, vr = {}, {}

    def pass_on(i, pieces=range(PIECES)):
        for p in pieces:
            part = pl.ds(p * HALF // PIECES, HALF // PIECES)
            for way, (sent, out, came, to, k) in enumerate(
                ((vl, sl, rl, left, S_LEFT), (vr, sr, rr, right, S_RIGHT))
            ):
                total = vp[pl.ds(ROWS * i + HALF * way + p * HALF // PIECES, HALF // PIECES), :]
                if i <= 5:
                    sent[i + 2, p].wait_recv()
                    total = total + decode(came[i + 2, part, :])
                out[i, part, :] = code(total)
                sent[i, p] = send(k + PIECES * i + p, out.at[i, part], came.at[i, part], to)

    def code_rows(dst, src, src_start, count):
        def some(k, carry):
            at = pl.multiple_of(k * 64, 64)
            dst[pl.ds(at, 64), :] = code(src[pl.ds(src_start + at, 64), :])
            return carry

        lax.fori_loop(0, count // 64, some, 0)

    gc = {}

    def text_to_sibling(h, yy):
        code_rows(core_out.at[h, yy], gp, 512 * h + 256 * yy + 128, 128)
        gc[h, yy] = send(G_CORE + 2 * h + yy, core_out.at[h, yy], core_in.at[h, yy], sibling)

    gy = {}

    def text_across(h):
        gc[h, 1].wait_recv()
        for k in range(2):
            at = pl.ds(64 * k, 64)
            y_out[h, at, :] = code(gp[pl.ds(512 * h + 256 + 64 * k, 64), :] + decode(core_in[h, 1, at, :]))
            gy[h, k] = send(G_Y + 2 * h + k, y_out.at[h, at], y_in.at[h, at], across)

    def text_sum(h, k):
        at = pl.ds(64 * k, 64)
        if k == 0:
            gc[h, 0].wait_recv()
        gy[h, k].wait_recv()
        near = gp[pl.ds(512 * h + 64 * k, 64), :]
        return near + decode(core_in[h, 0, at, :]) + decode(y_in[h, at, :])

    own_text.wait()
    own_image.wait()
    arrive(1)
    tc[0, 0].wait_recv()
    coefficients(0, 256, 0, 1)
    arrive(2)
    ty0.wait_recv()
    far_low, far_high = pl.ds(768, HALF), pl.ds(768 + HALF, HALF)
    tx1 = send(T_X + 1, tb.at[pl.ds(256 + HALF, HALF)], tb.at[far_high], up)
    tc[0, 1] = send(T_CORE + 1, tb.at[text(0, 1, 0)], tb.at[text(0, 1, 1)], sibling)
    tx.wait_recv()
    ty1 = send(T_Y + 1, tb.at[pl.ds(512, HALF)], tb.at[far_low], across)
    tc[1, 0] = send(T_CORE + 2, tb.at[text(1, 0, 0)], tb.at[text(1, 0, 1)], sibling)
    tc[0, 1].wait_recv()
    tc[1, 0].wait_recv()
    coefficients(0, 256, 1, 3)
    arrive(3)
    coefficients(256, 256, 0, 3)
    image_terms(0, 512, 0, 2)
    arrive(4)
    ty1.wait_recv()
    tc[1, 1] = send(T_CORE + 3, tb.at[far_low], tb.at[pl.ds(896, HALF)], sibling)
    tx1.wait_recv()
    tc[1, 2] = send(T_CORE + 4, tb.at[far_high], tb.at[pl.ds(896 + HALF, HALF)], sibling)
    tc[1, 1].wait_recv()
    tc[1, 2].wait_recv()
    coefficients(0, 256, 3, 4)
    coefficients(256, 256, 3, 4)
    image_terms(256, 256, 2, 4)
    arrive(5)
    coefficients(512, 256, 0, 4)
    image_terms(512, 256, 0, 4)
    arrive(6)
    coefficients(768, 128, 0, 4)
    image_terms(768, 128, 0, 4)
    pass_on(6)
    arrive(7)
    coefficients(896, 128, 0, 4)
    image_terms(896, 128, 0, 4)
    pass_on(7)
    gx = {}

    def text_down(k):
        at = pl.ds(64 * k, 64)
        x_out[at, :] = code(text_sum(1, k))
        gx[k] = send(G_X + k, x_out.at[at], x_in.at[at], down)

    text_terms(3, 0)
    pass_on(4, [0])
    text_terms(3, 1)
    text_to_sibling(1, 1)
    pass_on(4, [1])
    text_terms(2, 0)
    text_across(1)
    pass_on(5, [0])
    text_terms(2, 1)
    text_to_sibling(1, 0)
    pass_on(5, [1])
    text_terms(1, 0)
    pass_on(2, [0])
    text_terms(1, 1)
    text_to_sibling(0, 1)
    pass_on(2, [1])
    text_down(0)
    text_terms(0, 0)
    text_across(0)
    pass_on(3, [0])
    text_terms(0, 1)
    text_to_sibling(0, 0)
    pass_on(3, [1])
    text_down(1)
    image_terms(0, 256, 2, 4)
    pass_on(1)
    for p in range(PIECES):
        vl[2, p].wait_recv()
        vr[2, p].wait_recv()
    vp[low, :] = vp[low, :] + decode(rr[2])
    vp[high, :] = vp[high, :] + decode(rl[2])
    for k in range(2):
        gp[pl.ds(64 * k, 64), :] = text_sum(0, k)
    for k in range(2):
        at = pl.ds(64 * k, 64)
        gx[k].wait_recv()
        txt_ref[at, :] = (gp[at, :] + decode(x_in[at, :]))
    for p in range(PIECES):
        vl[1, p].wait_recv()
        vr[1, p].wait_recv()
    vis_ref[low, :] = (vp[low, :] + decode(rl[1]))
    vis_ref[high, :] = (vp[high, :] + decode(rr[1]))
    for copy in copies:
        if not any(copy is zr[1, p] or copy is zl[1, p] for p in range(PIECES)):
            copy.wait_send()


def per_device(images, texts, scale, bias):
    rows, width = images.shape
    bf16, f32 = jnp.bfloat16, jnp.float32
    out = jax.ShapeDtypeStruct((rows, width), f32)
    vmem = pl.BlockSpec(memory_space=pltpu.VMEM)
    hbm = pl.BlockSpec(memory_space=pltpu.HBM)
    smem = pl.BlockSpec(memory_space=pltpu.SMEM)
    visual, textual = pl.pallas_call(
        kernel,
        out_shape=(out, out),
        in_specs=[hbm, hbm, smem, smem],
        out_specs=(vmem, vmem),
        scratch_shapes=[
            pltpu.VMEM((1024, width), bf16),
            pltpu.VMEM((1024, width), bf16),
            pltpu.VMEM((1024, 1024), bf16),
            pltpu.VMEM((1024, 256), f32),
            pltpu.VMEM((1024, width), f32),
            pltpu.VMEM((1024, width), f32),
            pltpu.VMEM((8, HALF, width), bf16),
            pltpu.VMEM((8, HALF, width), bf16),
            pltpu.VMEM((8, HALF, width), bf16),
            pltpu.VMEM((8, HALF, width), bf16),
            pltpu.VMEM((2, 2, ROWS, width), bf16),
            pltpu.VMEM((2, 2, ROWS, width), bf16),
            pltpu.VMEM((2, ROWS, width), bf16),
            pltpu.VMEM((2, ROWS, width), bf16),
            pltpu.VMEM((ROWS, width), bf16),
            pltpu.VMEM((ROWS, width), bf16),
            pltpu.SemaphoreType.DMA((N_SEM,)),
            pltpu.SemaphoreType.DMA((N_SEM,)),
            pltpu.SemaphoreType.DMA((2,)),
        ],
        compiler_params=pltpu.CompilerParams(
            collective_id=0, has_side_effects=True, vmem_limit_bytes=48 * 1024 * 1024
        ),
        cost_estimate=pl.CostEstimate(
            flops=6 * 1024 * 1024 * width, bytes_accessed=12 * rows * width, transcendentals=2 * 1024 * 1024
        ),
    )(pltpu.with_memory_space_constraint(images, pltpu.HBM), pltpu.with_memory_space_constraint(texts, pltpu.HBM), scale, bias)
    return scale[0] * visual, scale[0] * textual


def solution(mesh):
    spec = P(("blk", "grp"), None)
    return jax.shard_map(
        per_device,
        mesh=mesh,
        in_specs=(spec, spec, P(), P()),
        out_specs=(spec, spec),
        check_vma=False,
    )
```

```python
import functools

import jax
import jax.numpy as jnp
from jax import lax
from jax.experimental import pallas as pl
from jax.experimental.pallas import tpu as pltpu
from jax.sharding import PartitionSpec as P

MESH = pl.DeviceIdType.MESH
LIFT = 2.0**18
TINY = 1e-37
LOG2E = 1.4426950408889634
HALF = 64
ROWS = 128
NT = (((1,), (1,)), ((), ()))
TN = (((0,), (0,)), ((), ()))

PIECES = 4
Z_RIGHT, Z_LEFT = 0, 8 * PIECES
S_RIGHT, S_LEFT = 16 * PIECES, 24 * PIECES
T_CORE = 32 * PIECES
T_Y, T_X = T_CORE + 5, T_CORE + 7
G_CORE = T_CORE + 9
G_Y, G_X = G_CORE + 4, G_CORE + 8
N_SEM = G_CORE + 10


def code(v):
    w = v * LIFT
    w = w * jnp.abs(w)
    w = w * jnp.abs(w)
    return w.astype(jnp.bfloat16)


def decode(u):
    u = u.astype(jnp.float32)
    r = lax.rsqrt(lax.rsqrt(jnp.maximum(jnp.abs(u), TINY))) * (1.0 / LIFT)
    return jnp.where(u < 0.0, -r, r)


def kernel(
    x_ref, t_ref, scale_ref, bias_ref, vis_ref, txt_ref,
    xb, tb, cb, db, vp, gp, sl, sr, rl, rr, core_out, core_in, y_out, y_in, x_out, x_in, ss, rs, own,
):
    blk = lax.axis_index("blk")
    grp = lax.axis_index("grp")
    z, y, core = grp // 4, (grp // 2) % 2, grp % 2
    right = (blk, ((z + 1) % 8) * 4 + y * 2 + core)
    left = (blk, ((z + 7) % 8) * 4 + y * 2 + core)
    across = (blk, z * 4 + (1 - y) * 2 + core)
    sibling = (blk, z * 4 + y * 2 + (1 - core))
    flip_down = 1 - (blk % 4 + 3) // 4
    up_blk = (blk + 1) % 8
    flip_up = 1 - (up_blk % 4 + 3) // 4
    down = ((blk + 7) % 8, z * 4 + ((y + flip_down) % 2) * 2 + core)
    up = (up_blk, z * 4 + ((y + flip_up) % 2) * 2 + core)

    barrier = pltpu.get_barrier_semaphore()
    for other in (right, left, across, sibling, down):
        pl.semaphore_signal(barrier, inc=1, device_id=other, device_id_type=MESH)
    own_image = pltpu.make_async_copy(x_ref, xb.at[pl.ds(0, ROWS)], own.at[0])
    own_text = pltpu.make_async_copy(t_ref, tb.at[pl.ds(0, ROWS)], own.at[1])
    own_image.start()
    own_text.start()
    pl.semaphore_wait(barrier, 5)

    copies = []

    def send(k, src, dst, device):
        copy = pltpu.make_async_remote_copy(
            src_ref=src, dst_ref=dst, send_sem=ss.at[k], recv_sem=rs.at[k],
            device_id=device, device_id_type=MESH,
        )
        copy.start()
        copies.append(copy)
        return copy

    low, high = pl.ds(0, HALF), pl.ds(HALF, HALF)

    def text(h, yy, cc):
        return pl.ds(512 * h + 256 * yy + 128 * cc, 128)

    zr, zl, tc = {}, {}, {}
    step = HALF // PIECES

    def go_round(i, p):
        at = pl.ds(ROWS * i + step * p, step)
        there = pl.ds(ROWS * i + HALF + step * p, step)
        if i <= 2:
            right_start, left_start = (0, HALF) if i == 1 else (HALF, 0)
            to_right, to_left = x_ref.at[pl.ds(right_start + step * p, step)], x_ref.at[pl.ds(left_start + step * p, step)]
        else:
            to_right = xb.at[pl.ds(ROWS * (i - 2) + step * p, step)]
            to_left = xb.at[pl.ds(ROWS * (i - 2) + HALF + step * p, step)]
        zr[i, p] = send(Z_RIGHT + PIECES * i + p, to_right, xb.at[at], right)
        zl[i, p] = send(Z_LEFT + PIECES * i + p, to_left, xb.at[there], left)

    for p in range(PIECES):
        go_round(1, p)
    ty0 = send(T_Y, t_ref, tb.at[text(0, 1, 0)], across)
    tx = send(T_X, t_ref, tb.at[text(1, 0, 0)], up)
    tc[0, 0] = send(T_CORE, t_ref, tb.at[text(0, 0, 1)], sibling)
    for p in range(PIECES):
        zr[1, p].wait_send()
        zl[1, p].wait_send()
        go_round(2, p)

    scale = scale_ref[0]
    slope = scale * (-LOG2E)
    shift = bias_ref[0] * LOG2E

    def arrive(i):
        for p in range(PIECES):
            zr[i, p].wait_recv()
            zl[i, p].wait_recv()
            if i + 2 <= 7:
                go_round(i + 2, p)

    def coefficients(start, rows, first, last):
        some = pl.ds(256 * first, 256 * (last - first))
        db[some, 0:rows] = lax.dot_general(
            tb[some, :], xb[start : start + rows, :], NT, preferred_element_type=jnp.float32
        )

        def tile(n, carry):
            texts = pl.ds(pl.multiple_of(n * 256, 256), 256)
            away = 1.0 + jnp.exp2(jnp.minimum(db[texts, 0:rows] * slope - shift, 126.0))
            c = pl.reciprocal(away, approx=True)
            c = c * (2.0 - away * c)
            if start == 0 and first == 0:
                row = lax.broadcasted_iota(jnp.int32, c.shape, 0) + n * 256
                col = lax.broadcasted_iota(jnp.int32, c.shape, 1)
                c = jnp.where((row == col) & (row < ROWS), c - 1.0, c)
            cb[texts, start : start + rows] = c.astype(jnp.bfloat16)
            return carry

        lax.fori_loop(first, last, tile, 0)

    def image_terms(start, rows, first, last):
        texts = pl.ds(256 * first, 256 * (last - first))
        term = lax.dot_general(
            cb[texts, start : start + rows], tb[texts, :], TN, preferred_element_type=jnp.float32
        )
        if first > 0:
            term = vp[start : start + rows, :] + term
        vp[start : start + rows, :] = term

    def text_terms(quarter):
        texts = pl.ds(256 * quarter, 256)
        gp[texts, :] = jnp.dot(cb[texts, :], xb[...], preferred_element_type=jnp.float32)

    vl, vr = {}, {}

    def pass_on(i):
        for p in range(PIECES):
            part = pl.ds(p * HALF // PIECES, HALF // PIECES)
            for way, (sent, out, came, to, k) in enumerate(
                ((vl, sl, rl, left, S_LEFT), (vr, sr, rr, right, S_RIGHT))
            ):
                total = vp[pl.ds(ROWS * i + HALF * way + p * HALF // PIECES, HALF // PIECES), :]
                if i <= 5:
                    sent[i + 2, p].wait_recv()
                    total = total + decode(came[i + 2, part, :])
                out[i, part, :] = code(total)
                sent[i, p] = send(k + PIECES * i + p, out.at[i, part], came.at[i, part], to)

    def code_rows(dst, src, src_start, count):
        def some(k, carry):
            at = pl.multiple_of(k * 64, 64)
            dst[pl.ds(at, 64), :] = code(src[pl.ds(src_start + at, 64), :])
            return carry

        lax.fori_loop(0, count // 64, some, 0)

    gc = {}

    def text_to_sibling(h, yy):
        code_rows(core_out.at[h, yy], gp, 512 * h + 256 * yy + 128, 128)
        gc[h, yy] = send(G_CORE + 2 * h + yy, core_out.at[h, yy], core_in.at[h, yy], sibling)

    gy = {}

    def text_across(h):
        gc[h, 1].wait_recv()
        for k in range(2):
            at = pl.ds(64 * k, 64)
            y_out[h, at, :] = code(gp[pl.ds(512 * h + 256 + 64 * k, 64), :] + decode(core_in[h, 1, at, :]))
            gy[h, k] = send(G_Y + 2 * h + k, y_out.at[h, at], y_in.at[h, at], across)

    def text_sum(h, k):
        at = pl.ds(64 * k, 64)
        if k == 0:
            gc[h, 0].wait_recv()
        gy[h, k].wait_recv()
        near = gp[pl.ds(512 * h + 64 * k, 64), :]
        return near + decode(core_in[h, 0, at, :]) + decode(y_in[h, at, :])

    own_text.wait()
    own_image.wait()
    arrive(1)
    tc[0, 0].wait_recv()
    coefficients(0, 256, 0, 1)
    arrive(2)
    ty0.wait_recv()
    far_low, far_high = pl.ds(768, HALF), pl.ds(768 + HALF, HALF)
    tx1 = send(T_X + 1, tb.at[pl.ds(256 + HALF, HALF)], tb.at[far_high], up)
    tc[0, 1] = send(T_CORE + 1, tb.at[text(0, 1, 0)], tb.at[text(0, 1, 1)], sibling)
    tx.wait_recv()
    ty1 = send(T_Y + 1, tb.at[pl.ds(512, HALF)], tb.at[far_low], across)
    tc[1, 0] = send(T_CORE + 2, tb.at[text(1, 0, 0)], tb.at[text(1, 0, 1)], sibling)
    tc[0, 1].wait_recv()
    tc[1, 0].wait_recv()
    coefficients(0, 256, 1, 3)
    arrive(3)
    coefficients(256, 256, 0, 3)
    image_terms(0, 512, 0, 2)
    arrive(4)
    ty1.wait_recv()
    tc[1, 1] = send(T_CORE + 3, tb.at[far_low], tb.at[pl.ds(896, HALF)], sibling)
    tx1.wait_recv()
    tc[1, 2] = send(T_CORE + 4, tb.at[far_high], tb.at[pl.ds(896 + HALF, HALF)], sibling)
    tc[1, 1].wait_recv()
    tc[1, 2].wait_recv()
    coefficients(0, 256, 3, 4)
    coefficients(256, 256, 3, 4)
    image_terms(256, 256, 2, 4)
    arrive(5)
    coefficients(512, 256, 0, 4)
    image_terms(512, 256, 0, 4)
    arrive(6)
    coefficients(768, 128, 0, 4)
    image_terms(768, 128, 0, 4)
    pass_on(6)
    arrive(7)
    coefficients(896, 128, 0, 4)
    image_terms(896, 128, 0, 4)
    pass_on(7)
    text_terms(3)
    text_to_sibling(1, 1)
    pass_on(4)
    text_across(1)
    text_terms(2)
    text_to_sibling(1, 0)
    pass_on(5)
    text_terms(1)
    text_to_sibling(0, 1)
    pass_on(2)
    gx = {}

    def text_down(k):
        at = pl.ds(64 * k, 64)
        x_out[at, :] = code(text_sum(1, k))
        gx[k] = send(G_X + k, x_out.at[at], x_in.at[at], down)

    text_down(0)
    text_across(0)
    text_terms(0)
    text_to_sibling(0, 0)
    pass_on(3)
    text_down(1)
    image_terms(0, 256, 2, 4)
    pass_on(1)
    for p in range(PIECES):
        vl[2, p].wait_recv()
        vr[2, p].wait_recv()
    vp[low, :] = vp[low, :] + decode(rr[2])
    vp[high, :] = vp[high, :] + decode(rl[2])
    for k in range(2):
        gp[pl.ds(64 * k, 64), :] = text_sum(0, k)
    for k in range(2):
        at = pl.ds(64 * k, 64)
        gx[k].wait_recv()
        txt_ref[at, :] = (gp[at, :] + decode(x_in[at, :]))
    for p in range(PIECES):
        vl[1, p].wait_recv()
        vr[1, p].wait_recv()
    vis_ref[low, :] = (vp[low, :] + decode(rl[1]))
    vis_ref[high, :] = (vp[high, :] + decode(rr[1]))
    for copy in copies:
        if not any(copy is zr[1, p] or copy is zl[1, p] for p in range(PIECES)):
            copy.wait_send()


def per_device(images, texts, scale, bias):
    rows, width = images.shape
    bf16, f32 = jnp.bfloat16, jnp.float32
    out = jax.ShapeDtypeStruct((rows, width), f32)
    vmem = pl.BlockSpec(memory_space=pltpu.VMEM)
    hbm = pl.BlockSpec(memory_space=pltpu.HBM)
    smem = pl.BlockSpec(memory_space=pltpu.SMEM)
    visual, textual = pl.pallas_call(
        kernel,
        out_shape=(out, out),
        in_specs=[hbm, hbm, smem, smem],
        out_specs=(vmem, vmem),
        scratch_shapes=[
            pltpu.VMEM((1024, width), bf16),
            pltpu.VMEM((1024, width), bf16),
            pltpu.VMEM((1024, 1024), bf16),
            pltpu.VMEM((1024, 256), f32),
            pltpu.VMEM((1024, width), f32),
            pltpu.VMEM((1024, width), f32),
            pltpu.VMEM((8, HALF, width), bf16),
            pltpu.VMEM((8, HALF, width), bf16),
            pltpu.VMEM((8, HALF, width), bf16),
            pltpu.VMEM((8, HALF, width), bf16),
            pltpu.VMEM((2, 2, ROWS, width), bf16),
            pltpu.VMEM((2, 2, ROWS, width), bf16),
            pltpu.VMEM((2, ROWS, width), bf16),
            pltpu.VMEM((2, ROWS, width), bf16),
            pltpu.VMEM((ROWS, width), bf16),
            pltpu.VMEM((ROWS, width), bf16),
            pltpu.SemaphoreType.DMA((N_SEM,)),
            pltpu.SemaphoreType.DMA((N_SEM,)),
            pltpu.SemaphoreType.DMA((2,)),
        ],
        compiler_params=pltpu.CompilerParams(
            collective_id=0, has_side_effects=True, vmem_limit_bytes=48 * 1024 * 1024
        ),
        cost_estimate=pl.CostEstimate(
            flops=6 * 1024 * 1024 * width, bytes_accessed=12 * rows * width, transcendentals=2 * 1024 * 1024
        ),
    )(pltpu.with_memory_space_constraint(images, pltpu.HBM), pltpu.with_memory_space_constraint(texts, pltpu.HBM), scale, bias)
    return scale[0] * visual, scale[0] * textual


def solution(mesh):
    spec = P(("blk", "grp"), None)
    return jax.shard_map(
        per_device,
        mesh=mesh,
        in_specs=(spec, spec, P(), P()),
        out_specs=(spec, spec),
        check_vma=False,
    )
```

```python
import functools

import jax
import jax.numpy as jnp
from jax import lax
from jax.experimental import pallas as pl
from jax.experimental.pallas import tpu as pltpu
from jax.sharding import PartitionSpec as P

MESH = pl.DeviceIdType.MESH
LIFT = 2.0**18
TINY = 1e-37
LOG2E = 1.4426950408889634
HALF = 64
ROWS = 128
NT = (((1,), (1,)), ((), ()))
TN = (((0,), (0,)), ((), ()))

Z_RIGHT, Z_LEFT = 0, 16
S_RIGHT, S_LEFT = 32, 48
T_CORE, T_Y, T_X = 64, 69, 71
G_CORE, G_Y, G_X = 73, 77, 81
N_SEM = 83
PIECES = 2


def code(v):
    w = v * LIFT
    w = w * jnp.abs(w)
    w = w * jnp.abs(w)
    return w.astype(jnp.bfloat16)


def decode(u):
    u = u.astype(jnp.float32)
    r = lax.rsqrt(lax.rsqrt(jnp.maximum(jnp.abs(u), TINY))) * (1.0 / LIFT)
    return jnp.where(u < 0.0, -r, r)


def kernel(
    x_ref, t_ref, scale_ref, bias_ref, vis_ref, txt_ref,
    xb, tb, cb, db, vp, gp, sl, sr, rl, rr, core_out, core_in, y_out, y_in, x_out, x_in, ss, rs, own,
):
    blk = lax.axis_index("blk")
    grp = lax.axis_index("grp")
    z, y, core = grp // 4, (grp // 2) % 2, grp % 2
    right = (blk, ((z + 1) % 8) * 4 + y * 2 + core)
    left = (blk, ((z + 7) % 8) * 4 + y * 2 + core)
    across = (blk, z * 4 + (1 - y) * 2 + core)
    sibling = (blk, z * 4 + y * 2 + (1 - core))
    flip_down = 1 - (blk % 4 + 3) // 4
    up_blk = (blk + 1) % 8
    flip_up = 1 - (up_blk % 4 + 3) // 4
    down = ((blk + 7) % 8, z * 4 + ((y + flip_down) % 2) * 2 + core)
    up = (up_blk, z * 4 + ((y + flip_up) % 2) * 2 + core)

    barrier = pltpu.get_barrier_semaphore()
    for other in (right, left, across, sibling, down):
        pl.semaphore_signal(barrier, inc=1, device_id=other, device_id_type=MESH)
    own_image = pltpu.make_async_copy(x_ref, xb.at[pl.ds(0, ROWS)], own.at[0])
    own_text = pltpu.make_async_copy(t_ref, tb.at[pl.ds(0, ROWS)], own.at[1])
    own_image.start()
    own_text.start()
    pl.semaphore_wait(barrier, 5)

    copies = []

    def send(k, src, dst, device):
        copy = pltpu.make_async_remote_copy(
            src_ref=src, dst_ref=dst, send_sem=ss.at[k], recv_sem=rs.at[k],
            device_id=device, device_id_type=MESH,
        )
        copy.start()
        copies.append(copy)
        return copy

    low, high = pl.ds(0, HALF), pl.ds(HALF, HALF)

    def text(h, yy, cc):
        return pl.ds(512 * h + 256 * yy + 128 * cc, 128)

    zr, zl, tc = {}, {}, {}
    step = HALF // PIECES

    def go_round(i, p):
        at = pl.ds(ROWS * i + step * p, step)
        there = pl.ds(ROWS * i + HALF + step * p, step)
        if i <= 2:
            right_start, left_start = (0, HALF) if i == 1 else (HALF, 0)
            to_right, to_left = x_ref.at[pl.ds(right_start + step * p, step)], x_ref.at[pl.ds(left_start + step * p, step)]
        else:
            to_right = xb.at[pl.ds(ROWS * (i - 2) + step * p, step)]
            to_left = xb.at[pl.ds(ROWS * (i - 2) + HALF + step * p, step)]
        zr[i, p] = send(Z_RIGHT + PIECES * i + p, to_right, xb.at[at], right)
        zl[i, p] = send(Z_LEFT + PIECES * i + p, to_left, xb.at[there], left)

    for p in range(PIECES):
        go_round(1, p)
    ty0 = send(T_Y, t_ref, tb.at[text(0, 1, 0)], across)
    tx = send(T_X, t_ref, tb.at[text(1, 0, 0)], up)
    tc[0, 0] = send(T_CORE, t_ref, tb.at[text(0, 0, 1)], sibling)
    for p in range(PIECES):
        zr[1, p].wait_send()
        zl[1, p].wait_send()
        go_round(2, p)

    scale = scale_ref[0]
    slope = scale * (-LOG2E)
    shift = bias_ref[0] * LOG2E

    def arrive(i):
        for p in range(PIECES):
            zr[i, p].wait_recv()
            zl[i, p].wait_recv()
            if i + 2 <= 7:
                go_round(i + 2, p)

    def coefficients(start, rows, first, last):
        some = pl.ds(256 * first, 256 * (last - first))
        db[some, 0:rows] = lax.dot_general(
            tb[some, :], xb[start : start + rows, :], NT, preferred_element_type=jnp.float32
        )

        def tile(n, carry):
            texts = pl.ds(pl.multiple_of(n * 256, 256), 256)
            away = 1.0 + jnp.exp2(jnp.minimum(db[texts, 0:rows] * slope - shift, 126.0))
            c = pl.reciprocal(away, approx=True)
            c = c * (2.0 - away * c)
            if start == 0 and first == 0:
                row = lax.broadcasted_iota(jnp.int32, c.shape, 0) + n * 256
                col = lax.broadcasted_iota(jnp.int32, c.shape, 1)
                c = jnp.where((row == col) & (row < ROWS), c - 1.0, c)
            cb[texts, start : start + rows] = c.astype(jnp.bfloat16)
            return carry

        lax.fori_loop(first, last, tile, 0)

    def image_terms(start, rows, first, last):
        texts = pl.ds(256 * first, 256 * (last - first))
        term = lax.dot_general(
            cb[texts, start : start + rows], tb[texts, :], TN, preferred_element_type=jnp.float32
        )
        if first > 0:
            term = vp[start : start + rows, :] + term
        vp[start : start + rows, :] = term

    def text_terms(quarter):
        texts = pl.ds(256 * quarter, 256)
        gp[texts, :] = jnp.dot(cb[texts, :], xb[...], preferred_element_type=jnp.float32)

    vl, vr = {}, {}

    def pieces(i):
        return 2 if i in (1, 3) else 1

    def pass_on(i):
        rows = HALF // pieces(i)
        for p in range(pieces(i)):
            part = pl.ds(p * rows, rows)
            for way, (sent, out, came, to, k) in enumerate(
                ((vl, sl, rl, left, S_LEFT), (vr, sr, rr, right, S_RIGHT))
            ):
                total = vp[pl.ds(ROWS * i + HALF * way + p * rows, rows), :]
                if i <= 5:
                    if p < pieces(i + 2):
                        sent[i + 2, p].wait_recv()
                    total = total + decode(came[i + 2, part, :])
                out[i, part, :] = code(total)
                sent[i, p] = send(k + PIECES * i + p, out.at[i, part], came.at[i, part], to)

    def code_rows(dst, src, src_start, count):
        def some(k, carry):
            at = pl.multiple_of(k * 64, 64)
            dst[pl.ds(at, 64), :] = code(src[pl.ds(src_start + at, 64), :])
            return carry

        lax.fori_loop(0, count // 64, some, 0)

    gc = {}

    def text_to_sibling(h, yy):
        code_rows(core_out.at[h, yy], gp, 512 * h + 256 * yy + 128, 128)
        gc[h, yy] = send(G_CORE + 2 * h + yy, core_out.at[h, yy], core_in.at[h, yy], sibling)

    gy = {}

    def text_across(h):
        gc[h, 1].wait_recv()
        for k in range(2):
            at = pl.ds(64 * k, 64)
            y_out[h, at, :] = code(gp[pl.ds(512 * h + 256 + 64 * k, 64), :] + decode(core_in[h, 1, at, :]))
            gy[h, k] = send(G_Y + 2 * h + k, y_out.at[h, at], y_in.at[h, at], across)

    def text_sum(h, k):
        at = pl.ds(64 * k, 64)
        if k == 0:
            gc[h, 0].wait_recv()
        gy[h, k].wait_recv()
        near = gp[pl.ds(512 * h + 64 * k, 64), :]
        return near + decode(core_in[h, 0, at, :]) + decode(y_in[h, at, :])

    own_text.wait()
    own_image.wait()
    arrive(1)
    tc[0, 0].wait_recv()
    coefficients(0, 256, 0, 1)
    arrive(2)
    ty0.wait_recv()
    far_low, far_high = pl.ds(768, HALF), pl.ds(768 + HALF, HALF)
    tx1 = send(T_X + 1, tb.at[pl.ds(256 + HALF, HALF)], tb.at[far_high], up)
    tc[0, 1] = send(T_CORE + 1, tb.at[text(0, 1, 0)], tb.at[text(0, 1, 1)], sibling)
    tx.wait_recv()
    ty1 = send(T_Y + 1, tb.at[pl.ds(512, HALF)], tb.at[far_low], across)
    tc[1, 0] = send(T_CORE + 2, tb.at[text(1, 0, 0)], tb.at[text(1, 0, 1)], sibling)
    tc[0, 1].wait_recv()
    tc[1, 0].wait_recv()
    coefficients(0, 256, 1, 3)
    arrive(3)
    coefficients(256, 256, 0, 3)
    image_terms(0, 512, 0, 2)
    arrive(4)
    ty1.wait_recv()
    tc[1, 1] = send(T_CORE + 3, tb.at[far_low], tb.at[pl.ds(896, HALF)], sibling)
    tx1.wait_recv()
    tc[1, 2] = send(T_CORE + 4, tb.at[far_high], tb.at[pl.ds(896 + HALF, HALF)], sibling)
    tc[1, 1].wait_recv()
    tc[1, 2].wait_recv()
    coefficients(0, 256, 3, 4)
    coefficients(256, 256, 3, 4)
    image_terms(256, 256, 2, 4)
    arrive(5)
    coefficients(512, 256, 0, 4)
    image_terms(512, 256, 0, 4)
    arrive(6)
    coefficients(768, 128, 0, 4)
    image_terms(768, 128, 0, 4)
    pass_on(6)
    arrive(7)
    coefficients(896, 128, 0, 4)
    image_terms(896, 128, 0, 4)
    pass_on(7)
    text_terms(3)
    text_to_sibling(1, 1)
    pass_on(4)
    text_across(1)
    text_terms(2)
    text_to_sibling(1, 0)
    pass_on(5)
    text_terms(1)
    text_to_sibling(0, 1)
    pass_on(2)
    gx = {}

    def text_down(k):
        at = pl.ds(64 * k, 64)
        x_out[at, :] = code(text_sum(1, k))
        gx[k] = send(G_X + k, x_out.at[at], x_in.at[at], down)

    text_down(0)
    text_across(0)
    text_terms(0)
    text_to_sibling(0, 0)
    pass_on(3)
    text_down(1)
    image_terms(0, 256, 2, 4)
    pass_on(1)
    vl[2, 0].wait_recv()
    vr[2, 0].wait_recv()
    vp[low, :] = vp[low, :] + decode(rr[2])
    vp[high, :] = vp[high, :] + decode(rl[2])
    for k in range(2):
        gp[pl.ds(64 * k, 64), :] = text_sum(0, k)
    for k in range(2):
        at = pl.ds(64 * k, 64)
        gx[k].wait_recv()
        txt_ref[at, :] = gp[at, :] + decode(x_in[at, :])
    for p in range(2):
        part, upper = pl.ds(32 * p, 32), pl.ds(HALF + 32 * p, 32)
        vl[1, p].wait_recv()
        vis_ref[part, :] = vp[part, :] + decode(rl[1, part, :])
        vr[1, p].wait_recv()
        vis_ref[upper, :] = vp[upper, :] + decode(rr[1, part, :])
    for copy in copies:
        if not any(copy is zr[1, p] or copy is zl[1, p] for p in range(PIECES)):
            copy.wait_send()


def per_device(images, texts, scale, bias):
    rows, width = images.shape
    bf16, f32 = jnp.bfloat16, jnp.float32
    out = jax.ShapeDtypeStruct((rows, width), f32)
    vmem = pl.BlockSpec(memory_space=pltpu.VMEM)
    hbm = pl.BlockSpec(memory_space=pltpu.HBM)
    smem = pl.BlockSpec(memory_space=pltpu.SMEM)
    visual, textual = pl.pallas_call(
        kernel,
        out_shape=(out, out),
        in_specs=[hbm, hbm, smem, smem],
        out_specs=(vmem, vmem),
        scratch_shapes=[
            pltpu.VMEM((1024, width), bf16),
            pltpu.VMEM((1024, width), bf16),
            pltpu.VMEM((1024, 1024), bf16),
            pltpu.VMEM((1024, 256), f32),
            pltpu.VMEM((1024, width), f32),
            pltpu.VMEM((1024, width), f32),
            pltpu.VMEM((8, HALF, width), bf16),
            pltpu.VMEM((8, HALF, width), bf16),
            pltpu.VMEM((8, HALF, width), bf16),
            pltpu.VMEM((8, HALF, width), bf16),
            pltpu.VMEM((2, 2, ROWS, width), bf16),
            pltpu.VMEM((2, 2, ROWS, width), bf16),
            pltpu.VMEM((2, ROWS, width), bf16),
            pltpu.VMEM((2, ROWS, width), bf16),
            pltpu.VMEM((ROWS, width), bf16),
            pltpu.VMEM((ROWS, width), bf16),
            pltpu.SemaphoreType.DMA((N_SEM,)),
            pltpu.SemaphoreType.DMA((N_SEM,)),
            pltpu.SemaphoreType.DMA((2,)),
        ],
        compiler_params=pltpu.CompilerParams(
            collective_id=0, has_side_effects=True, vmem_limit_bytes=48 * 1024 * 1024
        ),
        cost_estimate=pl.CostEstimate(
            flops=6 * 1024 * 1024 * width, bytes_accessed=12 * rows * width, transcendentals=2 * 1024 * 1024
        ),
    )(pltpu.with_memory_space_constraint(images, pltpu.HBM), pltpu.with_memory_space_constraint(texts, pltpu.HBM), scale, bias)
    return scale[0] * visual, scale[0] * textual


def solution(mesh):
    spec = P(("blk", "grp"), None)
    return jax.shard_map(
        per_device,
        mesh=mesh,
        in_specs=(spec, spec, P(), P()),
        out_specs=(spec, spec),
        check_vma=False,
    )
```

```python
import functools

import jax
import jax.numpy as jnp
from jax import lax
from jax.experimental import pallas as pl
from jax.experimental.pallas import tpu as pltpu
from jax.sharding import PartitionSpec as P

MESH = pl.DeviceIdType.MESH
LIFT = 2.0**18
TINY = 1e-37
LOG2E = 1.4426950408889634
HALF = 64
ROWS = 128
NT = (((1,), (1,)), ((), ()))
TN = (((0,), (0,)), ((), ()))

Z_RIGHT, Z_LEFT = 0, 16
S_RIGHT, S_LEFT = 32, 48
T_CORE, T_Y, T_X = 64, 69, 71
G_CORE, G_Y, G_X = 73, 77, 81
N_SEM = 83
PIECES = 2


def code(v):
    w = v * LIFT
    w = w * jnp.abs(w)
    w = w * jnp.abs(w)
    return w.astype(jnp.bfloat16)


def decode(u):
    u = u.astype(jnp.float32)
    r = lax.rsqrt(lax.rsqrt(jnp.maximum(jnp.abs(u), TINY))) * (1.0 / LIFT)
    return jnp.where(u < 0.0, -r, r)


def kernel(
    x_ref, t_ref, scale_ref, bias_ref, vis_ref, txt_ref,
    xb, tb, cb, db, vp, gp, sl, sr, rl, rr, core_out, core_in, y_out, y_in, x_out, x_in, ss, rs, own,
):
    blk = lax.axis_index("blk")
    grp = lax.axis_index("grp")
    z, y, core = grp // 4, (grp // 2) % 2, grp % 2
    right = (blk, ((z + 1) % 8) * 4 + y * 2 + core)
    left = (blk, ((z + 7) % 8) * 4 + y * 2 + core)
    across = (blk, z * 4 + (1 - y) * 2 + core)
    sibling = (blk, z * 4 + y * 2 + (1 - core))
    flip_down = 1 - (blk % 4 + 3) // 4
    up_blk = (blk + 1) % 8
    flip_up = 1 - (up_blk % 4 + 3) // 4
    down = ((blk + 7) % 8, z * 4 + ((y + flip_down) % 2) * 2 + core)
    up = (up_blk, z * 4 + ((y + flip_up) % 2) * 2 + core)

    barrier = pltpu.get_barrier_semaphore()
    for other in (right, left, across, sibling, down):
        pl.semaphore_signal(barrier, inc=1, device_id=other, device_id_type=MESH)
    own_image = pltpu.make_async_copy(x_ref, xb.at[pl.ds(0, ROWS)], own.at[0])
    own_text = pltpu.make_async_copy(t_ref, tb.at[pl.ds(0, ROWS)], own.at[1])
    own_image.start()
    own_text.start()
    pl.semaphore_wait(barrier, 5)

    copies = []

    def send(k, src, dst, device):
        copy = pltpu.make_async_remote_copy(
            src_ref=src, dst_ref=dst, send_sem=ss.at[k], recv_sem=rs.at[k],
            device_id=device, device_id_type=MESH,
        )
        copy.start()
        copies.append(copy)
        return copy

    low, high = pl.ds(0, HALF), pl.ds(HALF, HALF)

    def text(h, yy, cc):
        return pl.ds(512 * h + 256 * yy + 128 * cc, 128)

    zr, zl, tc = {}, {}, {}
    step = HALF // PIECES

    def go_round(i, p):
        at = pl.ds(ROWS * i + step * p, step)
        there = pl.ds(ROWS * i + HALF + step * p, step)
        if i <= 2:
            right_start, left_start = (0, HALF) if i == 1 else (HALF, 0)
            to_right, to_left = x_ref.at[pl.ds(right_start + step * p, step)], x_ref.at[pl.ds(left_start + step * p, step)]
        else:
            to_right = xb.at[pl.ds(ROWS * (i - 2) + step * p, step)]
            to_left = xb.at[pl.ds(ROWS * (i - 2) + HALF + step * p, step)]
        zr[i, p] = send(Z_RIGHT + PIECES * i + p, to_right, xb.at[at], right)
        zl[i, p] = send(Z_LEFT + PIECES * i + p, to_left, xb.at[there], left)

    for p in range(PIECES):
        go_round(1, p)
    ty0 = send(T_Y, t_ref, tb.at[text(0, 1, 0)], across)
    tx = send(T_X, t_ref, tb.at[text(1, 0, 0)], up)
    tc[0, 0] = send(T_CORE, t_ref, tb.at[text(0, 0, 1)], sibling)
    for p in range(PIECES):
        zr[1, p].wait_send()
        zl[1, p].wait_send()
        go_round(2, p)

    scale = scale_ref[0]
    slope = scale * (-LOG2E)
    shift = bias_ref[0] * LOG2E

    def arrive(i):
        for p in range(PIECES):
            zr[i, p].wait_recv()
            zl[i, p].wait_recv()
            if i + 2 <= 7:
                go_round(i + 2, p)

    def coefficients(start, rows, first, last):
        some = pl.ds(256 * first, 256 * (last - first))
        db[some, 0:rows] = lax.dot_general(
            tb[some, :], xb[start : start + rows, :], NT, preferred_element_type=jnp.float32
        )

        def tile(n, carry):
            texts = pl.ds(pl.multiple_of(n * 256, 256), 256)
            away = 1.0 + jnp.exp2(jnp.minimum(db[texts, 0:rows] * slope - shift, 126.0))
            c = pl.reciprocal(away, approx=True)
            c = c * (2.0 - away * c)
            if start == 0 and first == 0:
                row = lax.broadcasted_iota(jnp.int32, c.shape, 0) + n * 256
                col = lax.broadcasted_iota(jnp.int32, c.shape, 1)
                c = jnp.where((row == col) & (row < ROWS), c - 1.0, c)
            cb[texts, start : start + rows] = c.astype(jnp.bfloat16)
            return carry

        lax.fori_loop(first, last, tile, 0)

    def image_terms(start, rows, first, last):
        texts = pl.ds(256 * first, 256 * (last - first))
        term = lax.dot_general(
            cb[texts, start : start + rows], tb[texts, :], TN, preferred_element_type=jnp.float32
        )
        if first > 0:
            term = vp[start : start + rows, :] + term
        vp[start : start + rows, :] = term

    def text_terms(quarter):
        texts = pl.ds(256 * quarter, 256)
        gp[texts, :] = jnp.dot(cb[texts, :], xb[...], preferred_element_type=jnp.float32)

    vl, vr = {}, {}

    def pieces(i):
        return 2 if i in (1, 3) else 1

    def pass_on(i):
        rows = HALF // pieces(i)
        for p in range(pieces(i)):
            part = pl.ds(p * rows, rows)
            for way, (sent, out, came, to, k) in enumerate(
                ((vl, sl, rl, left, S_LEFT), (vr, sr, rr, right, S_RIGHT))
            ):
                total = vp[pl.ds(ROWS * i + HALF * way + p * rows, rows), :]
                if i <= 5:
                    if p < pieces(i + 2):
                        sent[i + 2, p].wait_recv()
                    total = total + decode(came[i + 2, part, :])
                out[i, part, :] = code(total)
                sent[i, p] = send(k + PIECES * i + p, out.at[i, part], came.at[i, part], to)

    def code_rows(dst, src, src_start, count):
        def some(k, carry):
            at = pl.multiple_of(k * 64, 64)
            dst[pl.ds(at, 64), :] = code(src[pl.ds(src_start + at, 64), :])
            return carry

        lax.fori_loop(0, count // 64, some, 0)

    gc = {}

    def text_to_sibling(h, yy):
        code_rows(core_out.at[h, yy], gp, 512 * h + 256 * yy + 128, 128)
        gc[h, yy] = send(G_CORE + 2 * h + yy, core_out.at[h, yy], core_in.at[h, yy], sibling)

    gy = {}

    def text_across(h):
        gc[h, 1].wait_recv()
        for k in range(2):
            at = pl.ds(64 * k, 64)
            y_out[h, at, :] = code(gp[pl.ds(512 * h + 256 + 64 * k, 64), :] + decode(core_in[h, 1, at, :]))
            gy[h, k] = send(G_Y + 2 * h + k, y_out.at[h, at], y_in.at[h, at], across)

    def text_sum(h, k):
        at = pl.ds(64 * k, 64)
        if k == 0:
            gc[h, 0].wait_recv()
        gy[h, k].wait_recv()
        near = gp[pl.ds(512 * h + 64 * k, 64), :]
        return near + decode(core_in[h, 0, at, :]) + decode(y_in[h, at, :])

    own_text.wait()
    own_image.wait()
    arrive(1)
    tc[0, 0].wait_recv()
    coefficients(0, 256, 0, 1)
    arrive(2)
    ty0.wait_recv()
    far_low, far_high = pl.ds(768, HALF), pl.ds(768 + HALF, HALF)
    tx1 = send(T_X + 1, tb.at[pl.ds(256 + HALF, HALF)], tb.at[far_high], up)
    tc[0, 1] = send(T_CORE + 1, tb.at[text(0, 1, 0)], tb.at[text(0, 1, 1)], sibling)
    tx.wait_recv()
    ty1 = send(T_Y + 1, tb.at[pl.ds(512, HALF)], tb.at[far_low], across)
    tc[1, 0] = send(T_CORE + 2, tb.at[text(1, 0, 0)], tb.at[text(1, 0, 1)], sibling)
    tc[0, 1].wait_recv()
    tc[1, 0].wait_recv()
    coefficients(0, 256, 1, 3)
    arrive(3)
    coefficients(256, 256, 0, 3)
    image_terms(0, 512, 0, 2)
    arrive(4)
    ty1.wait_recv()
    tc[1, 1] = send(T_CORE + 3, tb.at[far_low], tb.at[pl.ds(896, HALF)], sibling)
    tx1.wait_recv()
    tc[1, 2] = send(T_CORE + 4, tb.at[far_high], tb.at[pl.ds(896 + HALF, HALF)], sibling)
    tc[1, 1].wait_recv()
    tc[1, 2].wait_recv()
    coefficients(0, 256, 3, 4)
    coefficients(256, 256, 3, 4)
    image_terms(256, 256, 2, 4)
    arrive(5)
    coefficients(512, 256, 0, 4)
    image_terms(512, 256, 0, 4)
    arrive(6)
    coefficients(768, 128, 0, 4)
    image_terms(768, 128, 0, 4)
    pass_on(6)
    arrive(7)
    coefficients(896, 128, 0, 4)
    image_terms(896, 128, 0, 4)
    pass_on(7)
    text_terms(3)
    text_to_sibling(1, 1)
    pass_on(4)
    text_across(1)
    text_terms(2)
    text_to_sibling(1, 0)
    pass_on(5)
    text_terms(1)
    text_to_sibling(0, 1)
    pass_on(2)
    gx = {}

    def text_down(k):
        at = pl.ds(64 * k, 64)
        x_out[at, :] = code(text_sum(1, k))
        gx[k] = send(G_X + k, x_out.at[at], x_in.at[at], down)

    text_down(0)
    text_across(0)
    text_terms(0)
    text_to_sibling(0, 0)
    text_down(1)
    pass_on(3)
    image_terms(0, 256, 2, 4)
    pass_on(1)
    vl[2, 0].wait_recv()
    vr[2, 0].wait_recv()
    vp[low, :] = vp[low, :] + decode(rr[2])
    vp[high, :] = vp[high, :] + decode(rl[2])
    for k in range(2):
        gp[pl.ds(64 * k, 64), :] = text_sum(0, k)
    for k in range(2):
        at = pl.ds(64 * k, 64)
        gx[k].wait_recv()
        txt_ref[at, :] = gp[at, :] + decode(x_in[at, :])
    for p in range(2):
        part, upper = pl.ds(32 * p, 32), pl.ds(HALF + 32 * p, 32)
        vl[1, p].wait_recv()
        vis_ref[part, :] = vp[part, :] + decode(rl[1, part, :])
        vr[1, p].wait_recv()
        vis_ref[upper, :] = vp[upper, :] + decode(rr[1, part, :])
    for copy in copies:
        if not any(copy is zr[1, p] or copy is zl[1, p] for p in range(PIECES)):
            copy.wait_send()


def per_device(images, texts, scale, bias):
    rows, width = images.shape
    bf16, f32 = jnp.bfloat16, jnp.float32
    out = jax.ShapeDtypeStruct((rows, width), f32)
    vmem = pl.BlockSpec(memory_space=pltpu.VMEM)
    hbm = pl.BlockSpec(memory_space=pltpu.HBM)
    smem = pl.BlockSpec(memory_space=pltpu.SMEM)
    visual, textual = pl.pallas_call(
        kernel,
        out_shape=(out, out),
        in_specs=[hbm, hbm, smem, smem],
        out_specs=(vmem, vmem),
        scratch_shapes=[
            pltpu.VMEM((1024, width), bf16),
            pltpu.VMEM((1024, width), bf16),
            pltpu.VMEM((1024, 1024), bf16),
            pltpu.VMEM((1024, 256), f32),
            pltpu.VMEM((1024, width), f32),
            pltpu.VMEM((1024, width), f32),
            pltpu.VMEM((8, HALF, width), bf16),
            pltpu.VMEM((8, HALF, width), bf16),
            pltpu.VMEM((8, HALF, width), bf16),
            pltpu.VMEM((8, HALF, width), bf16),
            pltpu.VMEM((2, 2, ROWS, width), bf16),
            pltpu.VMEM((2, 2, ROWS, width), bf16),
            pltpu.VMEM((2, ROWS, width), bf16),
            pltpu.VMEM((2, ROWS, width), bf16),
            pltpu.VMEM((ROWS, width), bf16),
            pltpu.VMEM((ROWS, width), bf16),
            pltpu.SemaphoreType.DMA((N_SEM,)),
            pltpu.SemaphoreType.DMA((N_SEM,)),
            pltpu.SemaphoreType.DMA((2,)),
        ],
        compiler_params=pltpu.CompilerParams(
            collective_id=0, has_side_effects=True, vmem_limit_bytes=48 * 1024 * 1024
        ),
        cost_estimate=pl.CostEstimate(
            flops=6 * 1024 * 1024 * width, bytes_accessed=12 * rows * width, transcendentals=2 * 1024 * 1024
        ),
    )(pltpu.with_memory_space_constraint(images, pltpu.HBM), pltpu.with_memory_space_constraint(texts, pltpu.HBM), scale, bias)
    return scale[0] * visual, scale[0] * textual


def solution(mesh):
    spec = P(("blk", "grp"), None)
    return jax.shard_map(
        per_device,
        mesh=mesh,
        in_specs=(spec, spec, P(), P()),
        out_specs=(spec, spec),
        check_vma=False,
    )
```

```python
import functools

import jax
import jax.numpy as jnp
from jax import lax
from jax.experimental import pallas as pl
from jax.experimental.pallas import tpu as pltpu
from jax.sharding import PartitionSpec as P

MESH = pl.DeviceIdType.MESH
LIFT = 2.0**18
TINY = 1e-37
LOG2E = 1.4426950408889634
HALF = 64
ROWS = 128
NT = (((1,), (1,)), ((), ()))
TN = (((0,), (0,)), ((), ()))

Z_RIGHT, Z_LEFT = 0, 16
S_RIGHT, S_LEFT = 32, 48
T_CORE, T_Y, T_X = 64, 69, 71
G_CORE, G_Y, G_X = 73, 77, 81
N_SEM = 83
PIECES = 2


def code(v):
    w = v * LIFT
    w = w * jnp.abs(w)
    w = w * jnp.abs(w)
    return w.astype(jnp.bfloat16)


def decode(u):
    u = u.astype(jnp.float32)
    r = lax.rsqrt(lax.rsqrt(jnp.maximum(jnp.abs(u), TINY))) * (1.0 / LIFT)
    return jnp.where(u < 0.0, -r, r)


def kernel(
    x_ref, t_ref, scale_ref, bias_ref, vis_ref, txt_ref,
    xb, tb, cb, db, vp, gp, sl, sr, rl, rr, core_out, core_in, y_out, y_in, x_out, x_in, ss, rs, own,
):
    blk = lax.axis_index("blk")
    grp = lax.axis_index("grp")
    z, y, core = grp // 4, (grp // 2) % 2, grp % 2
    right = (blk, ((z + 1) % 8) * 4 + y * 2 + core)
    left = (blk, ((z + 7) % 8) * 4 + y * 2 + core)
    across = (blk, z * 4 + (1 - y) * 2 + core)
    sibling = (blk, z * 4 + y * 2 + (1 - core))
    flip_down = 1 - (blk % 4 + 3) // 4
    up_blk = (blk + 1) % 8
    flip_up = 1 - (up_blk % 4 + 3) // 4
    down = ((blk + 7) % 8, z * 4 + ((y + flip_down) % 2) * 2 + core)
    up = (up_blk, z * 4 + ((y + flip_up) % 2) * 2 + core)

    barrier = pltpu.get_barrier_semaphore()
    for other in (right, left, across, sibling, down):
        pl.semaphore_signal(barrier, inc=1, device_id=other, device_id_type=MESH)
    own_image = pltpu.make_async_copy(x_ref, xb.at[pl.ds(0, ROWS)], own.at[0])
    own_text = pltpu.make_async_copy(t_ref, tb.at[pl.ds(0, ROWS)], own.at[1])
    own_image.start()
    own_text.start()
    pl.semaphore_wait(barrier, 5)

    copies = []

    def send(k, src, dst, device):
        copy = pltpu.make_async_remote_copy(
            src_ref=src, dst_ref=dst, send_sem=ss.at[k], recv_sem=rs.at[k],
            device_id=device, device_id_type=MESH,
        )
        copy.start()
        copies.append(copy)
        return copy

    low, high = pl.ds(0, HALF), pl.ds(HALF, HALF)

    def text(h, yy, cc):
        return pl.ds(512 * h + 256 * yy + 128 * cc, 128)

    zr, zl, tc = {}, {}, {}
    step = HALF // PIECES

    def go_round(i, p):
        at = pl.ds(ROWS * i + step * p, step)
        there = pl.ds(ROWS * i + HALF + step * p, step)
        if i <= 2:
            right_start, left_start = (0, HALF) if i == 1 else (HALF, 0)
            to_right, to_left = x_ref.at[pl.ds(right_start + step * p, step)], x_ref.at[pl.ds(left_start + step * p, step)]
        else:
            to_right = xb.at[pl.ds(ROWS * (i - 2) + step * p, step)]
            to_left = xb.at[pl.ds(ROWS * (i - 2) + HALF + step * p, step)]
        zr[i, p] = send(Z_RIGHT + PIECES * i + p, to_right, xb.at[at], right)
        zl[i, p] = send(Z_LEFT + PIECES * i + p, to_left, xb.at[there], left)

    for p in range(PIECES):
        go_round(1, p)
    ty0 = send(T_Y, t_ref, tb.at[text(0, 1, 0)], across)
    tx = send(T_X, t_ref, tb.at[text(1, 0, 0)], up)
    tc[0, 0] = send(T_CORE, t_ref, tb.at[text(0, 0, 1)], sibling)
    for p in range(PIECES):
        go_round(2, p)

    scale = scale_ref[0]
    slope = scale * (-LOG2E)
    shift = bias_ref[0] * LOG2E

    def arrive(i):
        for p in range(PIECES):
            zr[i, p].wait_recv()
            zl[i, p].wait_recv()
            if i + 2 <= 7:
                go_round(i + 2, p)

    def coefficients(start, rows, first, last):
        some = pl.ds(256 * first, 256 * (last - first))
        db[some, 0:rows] = lax.dot_general(
            tb[some, :], xb[start : start + rows, :], NT, preferred_element_type=jnp.float32
        )

        def tile(n, carry):
            texts = pl.ds(pl.multiple_of(n * 256, 256), 256)
            away = 1.0 + jnp.exp2(jnp.minimum(db[texts, 0:rows] * slope - shift, 126.0))
            c = pl.reciprocal(away, approx=True)
            c = c * (2.0 - away * c)
            if start == 0 and first == 0:
                row = lax.broadcasted_iota(jnp.int32, c.shape, 0) + n * 256
                col = lax.broadcasted_iota(jnp.int32, c.shape, 1)
                c = jnp.where((row == col) & (row < ROWS), c - 1.0, c)
            cb[texts, start : start + rows] = c.astype(jnp.bfloat16)
            return carry

        lax.fori_loop(first, last, tile, 0)

    def image_terms(start, rows, first, last):
        texts = pl.ds(256 * first, 256 * (last - first))
        term = lax.dot_general(
            cb[texts, start : start + rows], tb[texts, :], TN, preferred_element_type=jnp.float32
        )
        if first > 0:
            term = vp[start : start + rows, :] + term
        vp[start : start + rows, :] = term

    def text_terms(quarter):
        texts = pl.ds(256 * quarter, 256)
        gp[texts, :] = jnp.dot(cb[texts, :], xb[...], preferred_element_type=jnp.float32)

    vl, vr = {}, {}

    def pieces(i):
        return 2 if i in (1, 3) else 1

    def pass_on(i):
        rows = HALF // pieces(i)
        for p in range(pieces(i)):
            part = pl.ds(p * rows, rows)
            for way, (sent, out, came, to, k) in enumerate(
                ((vl, sl, rl, left, S_LEFT), (vr, sr, rr, right, S_RIGHT))
            ):
                total = vp[pl.ds(ROWS * i + HALF * way + p * rows, rows), :]
                if i <= 5:
                    if p < pieces(i + 2):
                        sent[i + 2, p].wait_recv()
                    total = total + decode(came[i + 2, part, :])
                out[i, part, :] = code(total)
                sent[i, p] = send(k + PIECES * i + p, out.at[i, part], came.at[i, part], to)

    def code_rows(dst, src, src_start, count):
        def some(k, carry):
            at = pl.multiple_of(k * 64, 64)
            dst[pl.ds(at, 64), :] = code(src[pl.ds(src_start + at, 64), :])
            return carry

        lax.fori_loop(0, count // 64, some, 0)

    gc = {}

    def text_to_sibling(h, yy):
        code_rows(core_out.at[h, yy], gp, 512 * h + 256 * yy + 128, 128)
        gc[h, yy] = send(G_CORE + 2 * h + yy, core_out.at[h, yy], core_in.at[h, yy], sibling)

    gy = {}

    def text_across(h):
        gc[h, 1].wait_recv()
        for k in range(2):
            at = pl.ds(64 * k, 64)
            y_out[h, at, :] = code(gp[pl.ds(512 * h + 256 + 64 * k, 64), :] + decode(core_in[h, 1, at, :]))
            gy[h, k] = send(G_Y + 2 * h + k, y_out.at[h, at], y_in.at[h, at], across)

    def text_sum(h, k):
        at = pl.ds(64 * k, 64)
        if k == 0:
            gc[h, 0].wait_recv()
        gy[h, k].wait_recv()
        near = gp[pl.ds(512 * h + 64 * k, 64), :]
        return near + decode(core_in[h, 0, at, :]) + decode(y_in[h, at, :])

    own_text.wait()
    own_image.wait()
    arrive(1)
    tc[0, 0].wait_recv()
    coefficients(0, 256, 0, 1)
    arrive(2)
    ty0.wait_recv()
    far_low, far_high = pl.ds(768, HALF), pl.ds(768 + HALF, HALF)
    tx1 = send(T_X + 1, tb.at[pl.ds(256 + HALF, HALF)], tb.at[far_high], up)
    tc[0, 1] = send(T_CORE + 1, tb.at[text(0, 1, 0)], tb.at[text(0, 1, 1)], sibling)
    tx.wait_recv()
    ty1 = send(T_Y + 1, tb.at[pl.ds(512, HALF)], tb.at[far_low], across)
    tc[1, 0] = send(T_CORE + 2, tb.at[text(1, 0, 0)], tb.at[text(1, 0, 1)], sibling)
    tc[0, 1].wait_recv()
    tc[1, 0].wait_recv()
    coefficients(0, 256, 1, 3)
    arrive(3)
    coefficients(256, 256, 0, 3)
    image_terms(0, 512, 0, 2)
    arrive(4)
    ty1.wait_recv()
    tc[1, 1] = send(T_CORE + 3, tb.at[far_low], tb.at[pl.ds(896, HALF)], sibling)
    tx1.wait_recv()
    tc[1, 2] = send(T_CORE + 4, tb.at[far_high], tb.at[pl.ds(896 + HALF, HALF)], sibling)
    tc[1, 1].wait_recv()
    tc[1, 2].wait_recv()
    coefficients(0, 256, 3, 4)
    coefficients(256, 256, 3, 4)
    image_terms(256, 256, 2, 4)
    arrive(5)
    coefficients(512, 256, 0, 4)
    image_terms(512, 256, 0, 4)
    arrive(6)
    coefficients(768, 128, 0, 4)
    image_terms(768, 128, 0, 4)
    pass_on(6)
    arrive(7)
    coefficients(896, 128, 0, 4)
    image_terms(896, 128, 0, 4)
    pass_on(7)
    text_terms(3)
    text_to_sibling(1, 1)
    pass_on(4)
    text_across(1)
    text_terms(2)
    text_to_sibling(1, 0)
    pass_on(5)
    text_terms(1)
    text_to_sibling(0, 1)
    pass_on(2)
    gx = {}

    def text_down(k):
        at = pl.ds(64 * k, 64)
        x_out[at, :] = code(text_sum(1, k))
        gx[k] = send(G_X + k, x_out.at[at], x_in.at[at], down)

    text_down(0)
    text_across(0)
    text_terms(0)
    text_to_sibling(0, 0)
    pass_on(3)
    text_down(1)
    image_terms(0, 256, 2, 4)
    pass_on(1)
    vl[2, 0].wait_recv()
    vr[2, 0].wait_recv()
    vp[low, :] = vp[low, :] + decode(rr[2])
    vp[high, :] = vp[high, :] + decode(rl[2])
    for k in range(2):
        gp[pl.ds(64 * k, 64), :] = text_sum(0, k)
    for k in range(2):
        at = pl.ds(64 * k, 64)
        gx[k].wait_recv()
        txt_ref[at, :] = gp[at, :] + decode(x_in[at, :])
    for p in range(2):
        part, upper = pl.ds(32 * p, 32), pl.ds(HALF + 32 * p, 32)
        vl[1, p].wait_recv()
        vis_ref[part, :] = vp[part, :] + decode(rl[1, part, :])
        vr[1, p].wait_recv()
        vis_ref[upper, :] = vp[upper, :] + decode(rr[1, part, :])
    for copy in copies:
        copy.wait_send()


def per_device(images, texts, scale, bias):
    rows, width = images.shape
    bf16, f32 = jnp.bfloat16, jnp.float32
    out = jax.ShapeDtypeStruct((rows, width), f32)
    vmem = pl.BlockSpec(memory_space=pltpu.VMEM)
    hbm = pl.BlockSpec(memory_space=pltpu.HBM)
    smem = pl.BlockSpec(memory_space=pltpu.SMEM)
    visual, textual = pl.pallas_call(
        kernel,
        out_shape=(out, out),
        in_specs=[hbm, hbm, smem, smem],
        out_specs=(vmem, vmem),
        scratch_shapes=[
            pltpu.VMEM((1024, width), bf16),
            pltpu.VMEM((1024, width), bf16),
            pltpu.VMEM((1024, 1024), bf16),
            pltpu.VMEM((1024, 256), f32),
            pltpu.VMEM((1024, width), f32),
            pltpu.VMEM((1024, width), f32),
            pltpu.VMEM((8, HALF, width), bf16),
            pltpu.VMEM((8, HALF, width), bf16),
            pltpu.VMEM((8, HALF, width), bf16),
            pltpu.VMEM((8, HALF, width), bf16),
            pltpu.VMEM((2, 2, ROWS, width), bf16),
            pltpu.VMEM((2, 2, ROWS, width), bf16),
            pltpu.VMEM((2, ROWS, width), bf16),
            pltpu.VMEM((2, ROWS, width), bf16),
            pltpu.VMEM((ROWS, width), bf16),
            pltpu.VMEM((ROWS, width), bf16),
            pltpu.SemaphoreType.DMA((N_SEM,)),
            pltpu.SemaphoreType.DMA((N_SEM,)),
            pltpu.SemaphoreType.DMA((2,)),
        ],
        compiler_params=pltpu.CompilerParams(
            collective_id=0, has_side_effects=True, vmem_limit_bytes=48 * 1024 * 1024
        ),
        cost_estimate=pl.CostEstimate(
            flops=6 * 1024 * 1024 * width, bytes_accessed=12 * rows * width, transcendentals=2 * 1024 * 1024
        ),
    )(pltpu.with_memory_space_constraint(images, pltpu.HBM), pltpu.with_memory_space_constraint(texts, pltpu.HBM), scale, bias)
    return scale[0] * visual, scale[0] * textual


def solution(mesh):
    spec = P(("blk", "grp"), None)
    return jax.shard_map(
        per_device,
        mesh=mesh,
        in_specs=(spec, spec, P(), P()),
        out_specs=(spec, spec),
        check_vma=False,
    )
```

```python
import functools

import jax
import jax.numpy as jnp
from jax import lax
from jax.experimental import pallas as pl
from jax.experimental.pallas import tpu as pltpu
from jax.sharding import PartitionSpec as P

MESH = pl.DeviceIdType.MESH
LIFT = 2.0**18
TINY = 1e-37
LOG2E = 1.4426950408889634
HALF = 64
ROWS = 128
NT = (((1,), (1,)), ((), ()))
TN = (((0,), (0,)), ((), ()))

Z_RIGHT, Z_LEFT = 0, 16
S_RIGHT, S_LEFT = 32, 48
T_CORE, T_Y, T_X = 64, 69, 71
G_CORE, G_Y, G_X = 73, 77, 81
N_SEM = 83
PIECES = 2


def code(v):
    w = v * LIFT
    w = w * jnp.abs(w)
    w = w * jnp.abs(w)
    return w.astype(jnp.bfloat16)


def decode(u):
    u = u.astype(jnp.float32)
    r = lax.rsqrt(lax.rsqrt(jnp.maximum(jnp.abs(u), TINY))) * (1.0 / LIFT)
    return jnp.where(u < 0.0, -r, r)


def kernel(
    x_ref, t_ref, scale_ref, bias_ref, vis_ref, txt_ref,
    xb, tb, cb, db, vp, gp, sl, sr, rl, rr, core_out, core_in, y_out, y_in, x_out, x_in, ss, rs, own,
):
    blk = lax.axis_index("blk")
    grp = lax.axis_index("grp")
    z, y, core = grp // 4, (grp // 2) % 2, grp % 2
    right = (blk, ((z + 1) % 8) * 4 + y * 2 + core)
    left = (blk, ((z + 7) % 8) * 4 + y * 2 + core)
    across = (blk, z * 4 + (1 - y) * 2 + core)
    sibling = (blk, z * 4 + y * 2 + (1 - core))
    flip_down = 1 - (blk % 4 + 3) // 4
    up_blk = (blk + 1) % 8
    flip_up = 1 - (up_blk % 4 + 3) // 4
    down = ((blk + 7) % 8, z * 4 + ((y + flip_down) % 2) * 2 + core)
    up = (up_blk, z * 4 + ((y + flip_up) % 2) * 2 + core)

    barrier = pltpu.get_barrier_semaphore()
    for other in (right, left, across, sibling, down):
        pl.semaphore_signal(barrier, inc=1, device_id=other, device_id_type=MESH)
    own_image = pltpu.make_async_copy(x_ref, xb.at[pl.ds(0, ROWS)], own.at[0])
    own_text = pltpu.make_async_copy(t_ref, tb.at[pl.ds(0, ROWS)], own.at[1])
    own_image.start()
    own_text.start()
    pl.semaphore_wait(barrier, 5)

    copies = []

    def send(k, src, dst, device):
        copy = pltpu.make_async_remote_copy(
            src_ref=src, dst_ref=dst, send_sem=ss.at[k], recv_sem=rs.at[k],
            device_id=device, device_id_type=MESH,
        )
        copy.start()
        copies.append(copy)
        return copy

    low, high = pl.ds(0, HALF), pl.ds(HALF, HALF)

    def text(h, yy, cc):
        return pl.ds(512 * h + 256 * yy + 128 * cc, 128)

    zr, zl, tc = {}, {}, {}
    step = HALF // PIECES

    def go_round(i, p):
        at = pl.ds(ROWS * i + step * p, step)
        there = pl.ds(ROWS * i + HALF + step * p, step)
        if i <= 2:
            right_start, left_start = (0, HALF) if i == 1 else (HALF, 0)
            to_right, to_left = x_ref.at[pl.ds(right_start + step * p, step)], x_ref.at[pl.ds(left_start + step * p, step)]
        else:
            to_right = xb.at[pl.ds(ROWS * (i - 2) + step * p, step)]
            to_left = xb.at[pl.ds(ROWS * (i - 2) + HALF + step * p, step)]
        zr[i, p] = send(Z_RIGHT + PIECES * i + p, to_right, xb.at[at], right)
        zl[i, p] = send(Z_LEFT + PIECES * i + p, to_left, xb.at[there], left)

    for p in range(PIECES):
        go_round(1, p)
    ty0 = send(T_Y, t_ref, tb.at[text(0, 1, 0)], across)
    tx = send(T_X, t_ref, tb.at[text(1, 0, 0)], up)
    tc[0, 0] = send(T_CORE, t_ref, tb.at[text(0, 0, 1)], sibling)
    for p in range(PIECES):
        go_round(2, p)

    scale = scale_ref[0]
    slope = scale * (-LOG2E)
    shift = bias_ref[0] * LOG2E

    def arrive(i):
        for p in range(PIECES):
            zr[i, p].wait_recv()
            zl[i, p].wait_recv()
            if i + 2 <= 7:
                go_round(i + 2, p)

    def coefficients(start, rows, first, last):
        some = pl.ds(256 * first, 256 * (last - first))
        db[some, 0:rows] = lax.dot_general(
            tb[some, :], xb[start : start + rows, :], NT, preferred_element_type=jnp.float32
        )

        def tile(n, carry):
            texts = pl.ds(pl.multiple_of(n * 256, 256), 256)
            away = 1.0 + jnp.exp2(jnp.minimum(db[texts, 0:rows] * slope - shift, 126.0))
            c = pl.reciprocal(away, approx=True)
            c = c * (2.0 - away * c)
            if start == 0 and first == 0:
                row = lax.broadcasted_iota(jnp.int32, c.shape, 0) + n * 256
                col = lax.broadcasted_iota(jnp.int32, c.shape, 1)
                c = jnp.where((row == col) & (row < ROWS), c - 1.0, c)
            cb[texts, start : start + rows] = c.astype(jnp.bfloat16)
            return carry

        lax.fori_loop(first, last, tile, 0)

    def image_terms(start, rows, first, last):
        texts = pl.ds(256 * first, 256 * (last - first))
        term = lax.dot_general(
            cb[texts, start : start + rows], tb[texts, :], TN, preferred_element_type=jnp.float32
        )
        if first > 0:
            term = vp[start : start + rows, :] + term
        vp[start : start + rows, :] = term

    def text_terms(quarter):
        texts = pl.ds(256 * quarter, 256)
        gp[texts, :] = jnp.dot(cb[texts, :], xb[...], preferred_element_type=jnp.float32)

    vl, vr = {}, {}

    def pieces(i):
        return 2 if i in (1, 3) else 1

    def pass_on(i):
        rows = HALF // pieces(i)
        for p in range(pieces(i)):
            part = pl.ds(p * rows, rows)
            for way, (sent, out, came, to, k) in enumerate(
                ((vl, sl, rl, left, S_LEFT), (vr, sr, rr, right, S_RIGHT))
            ):
                total = vp[pl.ds(ROWS * i + HALF * way + p * rows, rows), :]
                if i <= 5:
                    if p < pieces(i + 2):
                        sent[i + 2, p].wait_recv()
                    total = total + decode(came[i + 2, part, :])
                out[i, part, :] = code(total)
                sent[i, p] = send(k + PIECES * i + p, out.at[i, part], came.at[i, part], to)

    def code_rows(dst, src, src_start, count):
        def some(k, carry):
            at = pl.multiple_of(k * 64, 64)
            dst[pl.ds(at, 64), :] = code(src[pl.ds(src_start + at, 64), :])
            return carry

        lax.fori_loop(0, count // 64, some, 0)

    gc = {}

    def text_to_sibling(h, yy):
        code_rows(core_out.at[h, yy], gp, 512 * h + 256 * yy + 128, 128)
        gc[h, yy] = send(G_CORE + 2 * h + yy, core_out.at[h, yy], core_in.at[h, yy], sibling)

    gy = {}

    def text_across(h):
        gc[h, 1].wait_recv()
        for k in range(2):
            at = pl.ds(64 * k, 64)
            y_out[h, at, :] = code(gp[pl.ds(512 * h + 256 + 64 * k, 64), :] + decode(core_in[h, 1, at, :]))
            gy[h, k] = send(G_Y + 2 * h + k, y_out.at[h, at], y_in.at[h, at], across)

    def text_sum(h, k):
        at = pl.ds(64 * k, 64)
        if k == 0:
            gc[h, 0].wait_recv()
        gy[h, k].wait_recv()
        near = gp[pl.ds(512 * h + 64 * k, 64), :]
        return near + decode(core_in[h, 0, at, :]) + decode(y_in[h, at, :])

    own_text.wait()
    own_image.wait()
    arrive(1)
    tc[0, 0].wait_recv()
    coefficients(0, 256, 0, 1)
    arrive(2)
    ty0.wait_recv()
    tc[0, 1] = send(T_CORE + 1, tb.at[text(0, 1, 0)], tb.at[text(0, 1, 1)], sibling)
    tx.wait_recv()
    ty1 = send(T_Y + 1, tb.at[text(1, 0, 0)], tb.at[text(1, 1, 0)], across)
    tc[1, 0] = send(T_CORE + 2, tb.at[text(1, 0, 0)], tb.at[text(1, 0, 1)], sibling)
    tc[0, 1].wait_recv()
    tc[1, 0].wait_recv()
    coefficients(0, 256, 1, 3)
    arrive(3)
    coefficients(256, 256, 0, 3)
    image_terms(0, 512, 0, 2)
    arrive(4)
    ty1.wait_recv()
    tc[1, 1] = send(T_CORE + 3, tb.at[text(1, 1, 0)], tb.at[text(1, 1, 1)], sibling)
    tc[1, 1].wait_recv()
    coefficients(0, 256, 3, 4)
    coefficients(256, 256, 3, 4)
    image_terms(256, 256, 2, 4)
    arrive(5)
    coefficients(512, 256, 0, 4)
    image_terms(512, 256, 0, 4)
    arrive(6)
    coefficients(768, 128, 0, 4)
    image_terms(768, 128, 0, 4)
    pass_on(6)
    arrive(7)
    coefficients(896, 128, 0, 4)
    image_terms(896, 128, 0, 4)
    pass_on(7)
    text_terms(3)
    text_to_sibling(1, 1)
    pass_on(4)
    text_across(1)
    text_terms(2)
    text_to_sibling(1, 0)
    pass_on(5)
    text_terms(1)
    text_to_sibling(0, 1)
    pass_on(2)
    gx = {}

    def text_down(k):
        at = pl.ds(64 * k, 64)
        x_out[at, :] = code(text_sum(1, k))
        gx[k] = send(G_X + k, x_out.at[at], x_in.at[at], down)

    text_down(0)
    text_across(0)
    text_terms(0)
    text_to_sibling(0, 0)
    pass_on(3)
    text_down(1)
    image_terms(0, 256, 2, 4)
    pass_on(1)
    vl[2, 0].wait_recv()
    vr[2, 0].wait_recv()
    vp[low, :] = vp[low, :] + decode(rr[2])
    vp[high, :] = vp[high, :] + decode(rl[2])
    for k in range(2):
        gp[pl.ds(64 * k, 64), :] = text_sum(0, k)
    for k in range(2):
        at = pl.ds(64 * k, 64)
        gx[k].wait_recv()
        txt_ref[at, :] = gp[at, :] + decode(x_in[at, :])
    for p in range(2):
        part, upper = pl.ds(32 * p, 32), pl.ds(HALF + 32 * p, 32)
        vl[1, p].wait_recv()
        vis_ref[part, :] = vp[part, :] + decode(rl[1, part, :])
        vr[1, p].wait_recv()
        vis_ref[upper, :] = vp[upper, :] + decode(rr[1, part, :])
    for copy in copies:
        copy.wait_send()


def per_device(images, texts, scale, bias):
    rows, width = images.shape
    bf16, f32 = jnp.bfloat16, jnp.float32
    out = jax.ShapeDtypeStruct((rows, width), f32)
    vmem = pl.BlockSpec(memory_space=pltpu.VMEM)
    hbm = pl.BlockSpec(memory_space=pltpu.HBM)
    smem = pl.BlockSpec(memory_space=pltpu.SMEM)
    visual, textual = pl.pallas_call(
        kernel,
        out_shape=(out, out),
        in_specs=[hbm, hbm, smem, smem],
        out_specs=(vmem, vmem),
        scratch_shapes=[
            pltpu.VMEM((1024, width), bf16),
            pltpu.VMEM((1024, width), bf16),
            pltpu.VMEM((1024, 1024), bf16),
            pltpu.VMEM((1024, 256), f32),
            pltpu.VMEM((1024, width), f32),
            pltpu.VMEM((1024, width), f32),
            pltpu.VMEM((8, HALF, width), bf16),
            pltpu.VMEM((8, HALF, width), bf16),
            pltpu.VMEM((8, HALF, width), bf16),
            pltpu.VMEM((8, HALF, width), bf16),
            pltpu.VMEM((2, 2, ROWS, width), bf16),
            pltpu.VMEM((2, 2, ROWS, width), bf16),
            pltpu.VMEM((2, ROWS, width), bf16),
            pltpu.VMEM((2, ROWS, width), bf16),
            pltpu.VMEM((ROWS, width), bf16),
            pltpu.VMEM((ROWS, width), bf16),
            pltpu.SemaphoreType.DMA((N_SEM,)),
            pltpu.SemaphoreType.DMA((N_SEM,)),
            pltpu.SemaphoreType.DMA((2,)),
        ],
        compiler_params=pltpu.CompilerParams(
            collective_id=0, has_side_effects=True, vmem_limit_bytes=48 * 1024 * 1024
        ),
        cost_estimate=pl.CostEstimate(
            flops=6 * 1024 * 1024 * width, bytes_accessed=12 * rows * width, transcendentals=2 * 1024 * 1024
        ),
    )(pltpu.with_memory_space_constraint(images, pltpu.HBM), pltpu.with_memory_space_constraint(texts, pltpu.HBM), scale, bias)
    return scale[0] * visual, scale[0] * textual


def solution(mesh):
    spec = P(("blk", "grp"), None)
    return jax.shard_map(
        per_device,
        mesh=mesh,
        in_specs=(spec, spec, P(), P()),
        out_specs=(spec, spec),
        check_vma=False,
    )
```
